32 devices in a mesh: seq: 8 (over z, y), tp: 4 (over x, core).
Axes of the slice: x: 2, y: 2, z: 4, core: 2. Of those that a mesh axis runs over, the one named last changes fastest.
Arguments:
- latent: bfloat16 [2048, 3072], P(('seq', 'tp')), may hold values from -6 to 6
- queries: bfloat16 [2048, 1536], P('seq', 'tp'), may hold values from -40 to 40
- key_vectors: bfloat16 [2048, 1536], P('seq', 'tp'), may hold values from -40 to 40
- value_vectors: bfloat16 [2048, 1536], P('seq', 'tp'), may hold values from -6 to 6
- proj_weight: bfloat16 [1536, 3072], P('tp'), may hold values from -0.15625 to 0.15625
- gate_scale: float32 [8, 3072], replicated, may hold values from -2 to 2
- text_length: int32 [8], replicated, may hold values from 64 to 128, as said below
- split_table: int32 [8, 1], replicated, may hold values from 64 to 256, as said below
Outputs:
- updated: bfloat16 [2048, 3072], P(('seq', 'tp'))
The draws below stay inside these ranges and needn't reach their ends.
Inputs may be any that keep to these rules, and one draw needn't show every extreme that they name: `text_length`: some request has exactly 128 text tokens; text tokens are the first positions of a request. `split_table`: live slots of a device are its first ones; some request has an index of its group with all 256 slots live.
All inputs are finite; a program needn't handle non-finite values.
Results may differ from the reference program's by a relative error of at most 0.0075.
Values may be sent and summed in bfloat16 or wider, within the bound.
A program may use at most 64 MiB of HBM per device.

```python
import math
import jax
import jax.numpy as jnp
from jax import lax

D = 3072
HEADS = 12
HEAD_DIM = 128
TOK_DEV = 256
ITEMS = 8
TEXT_MOST = 128
GROUP = 1
SLOTS = 2048


def drawn_draw(key, first):
    drawn = jax.random.normal(jax.random.fold_in(key, first), (SLOTS, HEADS, HEAD_DIM), jnp.float32)
    return jnp.clip(drawn, -40.0, 40.0).reshape(SLOTS, HEADS * HEAD_DIM)


def draw_queries(key, part):
    return drawn_draw(key, 1).astype(jnp.bfloat16)


def draw_key_vectors(key, part):
    return drawn_draw(key, 4).astype(jnp.bfloat16)


def draw_text_length(key, part):
    drawn = jax.random.randint(jax.random.fold_in(key, 21), (ITEMS,), TEXT_MOST // 2, TEXT_MOST + 1)
    chosen = jax.random.randint(jax.random.fold_in(key, 22), (1,), 0, ITEMS)
    return jnp.where(jnp.arange(ITEMS) == chosen, TEXT_MOST, drawn).astype(jnp.int32)


def draw_split_table(key, part):
    drawn = jax.random.randint(jax.random.fold_in(key, 31), (ITEMS, GROUP), TOK_DEV // 4, TOK_DEV + 1)
    chosen = jax.random.randint(jax.random.fold_in(key, 32), (1,), 0, ITEMS * GROUP)
    flat_index = jnp.arange(ITEMS * GROUP, dtype=jnp.int32).reshape(ITEMS, GROUP)
    return jnp.where(flat_index == chosen, TOK_DEV, drawn).astype(jnp.int32)


def block_scale(own_key, extent, cuts, smallest, high):
    loudness, own = 1.0, jax.random.fold_in(own_key, 6)
    for dim, parts in cuts:
        draws = jnp.exp(jax.random.uniform(jax.random.fold_in(own, dim), (parts,), jnp.float32, smallest / len(cuts), high / len(cuts)))
        loudness = loudness * jnp.repeat(draws, extent[dim] // parts).reshape([-1 if axis == dim else 1 for axis in range(len(extent))])
    return loudness


def noise(rng, extent, spread, limit, split=(), held_as=jnp.bfloat16):
    array = spread * jax.random.normal(rng, extent, jnp.float32)
    if split:
        array = array * block_scale(rng, extent, split, -0.22, 0.18)
    return jnp.clip(array, -limit, limit).astype(held_as)


def setup_inputs(seed: int = 0) -> dict:
    arg_keys = jax.random.split(jax.random.key(seed), 9)
    latent = noise(arg_keys[0], (SLOTS, D), 1.0, 6.0, ((0, 32),))
    queries = draw_queries(jax.random.fold_in(arg_keys[8], 71), 0)
    key_vectors = draw_key_vectors(jax.random.fold_in(arg_keys[8], 71), 0)
    value_vectors = noise(arg_keys[3], (SLOTS, HEADS * HEAD_DIM), 1.0, 6.0, ((0, 8), (1, 4)))
    proj_weight = noise(arg_keys[4], (HEADS * HEAD_DIM, D), (HEADS * HEAD_DIM) ** -0.5, 0.15625, ((0, 4),))
    gate_scale = jnp.clip(jax.random.uniform(arg_keys[5], (ITEMS, D), jnp.float32, -2.0, 2.0), -2.0, 2.0)
    text_length = draw_text_length(jax.random.fold_in(arg_keys[8], 71), 0)
    split_table = draw_split_table(jax.random.fold_in(arg_keys[8], 71), 0)
    return {"latent": latent, "queries": queries, "key_vectors": key_vectors, "value_vectors": value_vectors, "proj_weight": proj_weight, "gate_scale": gate_scale, "text_length": text_length, "split_table": split_table}


def attend_head(query_head, key_head, value_head, key_live):
    scores = jnp.dot(query_head, key_head.T, preferred_element_type=jnp.float32) * (1.0 / math.sqrt(HEAD_DIM))
    scores = jnp.where(key_live[None, :], scores, -1e+30)
    top_score = lax.optimization_barrier(jnp.max(scores, axis=1, keepdims=True))
    weights = jnp.exp(scores - top_score) * key_live[None, :].astype(jnp.float32)
    weight_total = lax.optimization_barrier(jnp.sum(weights, axis=1, keepdims=True))
    summed = jnp.dot(weights.astype(jnp.bfloat16), value_head, preferred_element_type=jnp.float32)
    return (summed / weight_total).astype(jnp.bfloat16)

def reference(latent, queries, key_vectors, value_vectors, proj_weight, gate_scale, text_length, split_table):
    item_span = GROUP * TOK_DEV
    slot_index = jnp.arange(TOK_DEV, dtype=jnp.int32)
    key_live = slot_index[None, None, :] < split_table[:, :, None]
    offsets = jnp.cumsum(split_table, axis=1) - split_table
    position = offsets[:, :, None] + slot_index[None, None, :]
    image_mask = key_live & (position >= text_length[:, None, None])
    key_live = key_live.reshape(ITEMS, item_span)
    image_mask = image_mask.reshape(ITEMS, item_span)

    def heads_first(matrix):
        return matrix.reshape(item_span, HEADS, HEAD_DIM).transpose(1, 0, 2)

    def per_item(inputs):
        query_item, key_item, value_item, latent_item, live_item, image_item, gate_item = inputs

        def per_head(head_parts):
            return attend_head(head_parts[0], head_parts[1], head_parts[2], live_item)
        attended = lax.map(per_head, (heads_first(query_item), heads_first(key_item), heads_first(value_item)))
        attended = attended.transpose(1, 0, 2).reshape(item_span, HEADS * HEAD_DIM)
        projected = jnp.dot(attended, proj_weight, preferred_element_type=jnp.float32)
        residual_base = latent_item.astype(jnp.float32)
        return jnp.where(image_item[:, None], residual_base + gate_item[None, :] * projected, residual_base).astype(jnp.bfloat16)
    result = lax.map(per_item, (queries.reshape(ITEMS, item_span, HEADS * HEAD_DIM), key_vectors.reshape(ITEMS, item_span, HEADS * HEAD_DIM), value_vectors.reshape(ITEMS, item_span, HEADS * HEAD_DIM), latent.reshape(ITEMS, item_span, D), key_live, image_mask, gate_scale))
    return result.reshape(ITEMS * item_span, D)
```

```python
import functools
import math

import jax
import jax.numpy as jnp
from jax import lax
from jax.experimental import pallas as pl
from jax.experimental.pallas import tpu as pltpu
from jax.sharding import PartitionSpec as P

HEAD_DIM = 128
LEAST_TEXT = 64
CHUNKS = 6
MESH = pl.DeviceIdType.MESH


def local_kernel(
    latent, queries, key_vectors, value_vectors, proj_weight, gate_scale, text_length, split_table,
    out,
    q_buf, k_buf, v_buf, w_buf, latent_buf, gate_buf, text_buf, table_buf,
    attended, mate_send, mate_recv, kept, far_send, far_recv, near_send, near_recv, own,
    q_sem, kv_sem, w_sem, small_sem,
    mate_sems, far_sems, near_sems,
):
    seq, tp = lax.axis_index("seq"), lax.axis_index("tp")
    core = lax.rem(tp, 2)
    mate = tp + 1 - 2 * core
    far = lax.rem(tp + 2, 4)
    far_mate = lax.rem(mate + 2, 4)
    tokens, width = q_buf.shape
    block = tokens // 4
    heads = width // HEAD_DIM
    columns = w_buf.shape[2]

    barrier = pltpu.get_barrier_semaphore()
    for other in (mate, far):
        pl.semaphore_signal(barrier, inc=1, device_id=(seq, other), device_id_type=MESH)

    q_copies = []
    for place, owner in enumerate((far_mate, far, mate, tp)):
        q_copies.append(
            pltpu.make_async_copy(
                queries.at[pl.ds(pl.multiple_of(owner * block, block), block)],
                q_buf.at[pl.ds(place * block, block)],
                q_sem.at[place],
            )
        )
    k_copy = pltpu.make_async_copy(key_vectors, k_buf, kv_sem.at[0])
    v_copy = pltpu.make_async_copy(value_vectors, v_buf, kv_sem.at[1])
    table_copy = pltpu.make_async_copy(split_table, table_buf, small_sem.at[0])
    text_copy = pltpu.make_async_copy(text_length, text_buf, small_sem.at[1])
    gate_copy = pltpu.make_async_copy(gate_scale, gate_buf, small_sem.at[2])
    latent_copy = pltpu.make_async_copy(latent, latent_buf, small_sem.at[3])
    w_copies = [
        pltpu.make_async_copy(proj_weight.at[:, pl.ds(i * columns, columns)], w_buf.at[i], w_sem.at[i])
        for i in range(CHUNKS)
    ]
    for copy in (table_copy, k_copy, *q_copies, v_copy, *w_copies, text_copy, gate_copy, latent_copy):
        copy.start()

    def remote(source, target, sems, i, other):
        return pltpu.make_async_remote_copy(
            src_ref=source.at[i],
            dst_ref=target.at[i],
            send_sem=sems.at[0, i],
            recv_sem=sems.at[1, i],
            device_id=(seq, other),
            device_id_type=MESH,
        )

    to_mate = [remote(mate_send, mate_recv, mate_sems, i, mate) for i in range(CHUNKS)]
    to_far = [remote(far_send, far_recv, far_sems, i, far) for i in range(CHUNKS)]
    to_owner = [remote(near_send, near_recv, near_sems, i, mate) for i in range(CHUNKS)]

    table_copy.wait()
    count = table_buf[seq]
    key_live = lax.broadcasted_iota(jnp.int32, (1, tokens), 1) < count
    score_scale = 1.0 / math.sqrt(HEAD_DIM)

    def attend(first):
        rows = pl.ds(first, 2 * block)
        for head in range(heads):
            part = pl.ds(head * HEAD_DIM, HEAD_DIM)
            scores = lax.dot_general(
                q_buf[rows, part], k_buf[:, part], (((1,), (1,)), ((), ())),
                preferred_element_type=jnp.float32,
            )
            scores = jnp.where(key_live, scores * score_scale, -1e30)
            top = jnp.max(scores, axis=1, keepdims=True)
            weights = jnp.exp(scores - top)
            total = jnp.sum(weights, axis=1, keepdims=True)
            summed = jnp.dot(
                weights.astype(jnp.bfloat16), v_buf[:, part], preferred_element_type=jnp.float32
            )
            attended[rows, part] = (summed / total).astype(jnp.bfloat16)

    k_copy.wait()
    for copy in q_copies:
        copy.wait()
    v_copy.wait()
    attend(0)

    for i in range(CHUNKS + 1):
        if i < CHUNKS:
            w_copies[i].wait()
            share = jnp.dot(
                attended[pl.ds(0, 2 * block), :], w_buf[i], preferred_element_type=jnp.float32
            )
            mate_send[i] = share[:block].astype(jnp.bfloat16)
            kept[i] = share[block:]
            if i == 0:
                pl.semaphore_wait(barrier, 2)

            @pl.when(tp != 3)
            def _():
                to_mate[i].start()

        if i >= 1:
            j = i - 1

            @pl.when(tp != 2)
            def _():
                to_mate[j].wait_recv()
                far_send[j] = (kept[j] + mate_recv[j].astype(jnp.float32)).astype(jnp.bfloat16)
                to_far[j].start()

    attend(2 * block)
    for i in range(CHUNKS):
        share = jnp.dot(
            attended[pl.ds(2 * block, 2 * block), :], w_buf[i], preferred_element_type=jnp.float32
        )
        near_send[i] = share[:block].astype(jnp.bfloat16)
        own[i] = share[block:]

        @pl.when(tp != 1)
        def _():
            to_owner[i].start()

    text_copy.wait()
    gate_copy.wait()
    latent_copy.wait()
    text = text_buf[seq]
    position = tp * block + lax.broadcasted_iota(jnp.int32, (block, 1), 0)
    image = (position >= text) & (position < count)

    @pl.when(tp == 0)
    def _():
        out[...] = latent_buf[...]

    @pl.when(tp != 0)
    def _():
        for i in range(CHUNKS):
            part = pl.ds(i * columns, columns)
            to_owner[i].wait_recv()
            projected = own[i] + near_recv[i].astype(jnp.float32)
            to_far[i].wait_recv()
            projected = projected + far_recv[i].astype(jnp.float32)
            base = latent_buf[:, part].astype(jnp.float32)
            gate = gate_buf[pl.ds(seq, 1), part]
            out[:, part] = jnp.where(image, base + gate * projected, base).astype(jnp.bfloat16)

    for copies, idle in ((to_mate, 3), (to_far, 2), (to_owner, 1)):

        @pl.when(tp != idle)
        def _():
            for copy in copies:
                copy.wait_send()


def on_device_local(
    latent, queries, key_vectors, value_vectors, proj_weight, gate_scale, text_length, split_table
):
    tokens, width = queries.shape
    model = proj_weight.shape[1]
    block, columns = tokens // 4, model // CHUNKS
    in_hbm = pl.BlockSpec(memory_space=pltpu.HBM)
    blocks16 = pltpu.VMEM((CHUNKS, block, columns), jnp.bfloat16)
    blocks32 = pltpu.VMEM((CHUNKS, block, columns), jnp.float32)
    return pl.pallas_call(
        local_kernel,
        out_shape=jax.ShapeDtypeStruct(latent.shape, latent.dtype),
        in_specs=[in_hbm] * 8,
        out_specs=pl.BlockSpec(memory_space=pltpu.VMEM),
        scratch_shapes=[
            pltpu.VMEM((tokens, width), jnp.bfloat16),
            pltpu.VMEM((tokens, width), jnp.bfloat16),
            pltpu.VMEM((tokens, width), jnp.bfloat16),
            pltpu.VMEM((CHUNKS, width, columns), jnp.bfloat16),
            pltpu.VMEM(latent.shape, jnp.bfloat16),
            pltpu.VMEM(gate_scale.shape, jnp.float32),
            pltpu.SMEM(text_length.shape, jnp.int32),
            pltpu.SMEM((split_table.size,), jnp.int32),
            pltpu.VMEM((tokens, width), jnp.bfloat16),
            blocks16, blocks16, blocks32, blocks16, blocks16, blocks16, blocks16, blocks32,
            pltpu.SemaphoreType.DMA((4,)),
            pltpu.SemaphoreType.DMA((2,)),
            pltpu.SemaphoreType.DMA((CHUNKS,)),
            pltpu.SemaphoreType.DMA((4,)),
            pltpu.SemaphoreType.DMA((2, CHUNKS)),
            pltpu.SemaphoreType.DMA((2, CHUNKS)),
            pltpu.SemaphoreType.DMA((2, CHUNKS)),
        ],
        compiler_params=pltpu.CompilerParams(
            collective_id=0, has_side_effects=True, vmem_limit_bytes=64 * 2**20
        ),
        cost_estimate=pl.CostEstimate(
            flops=2 * tokens * width * (model + 2 * tokens), bytes_accessed=4 * 2**20, transcendentals=0
        ),
    )(latent, queries, key_vectors, value_vectors, proj_weight, gate_scale, text_length, split_table.reshape(-1))


def shortened(shard):
    return jax.tree.map(lambda a: a.astype(jnp.bfloat16) if a.dtype == jnp.float32 else a, shard)


def from_partner(block, axis, stride):
    count = lax.axis_size(axis)
    route = []
    for low in range(count):
        high = low | 1 << stride
        if high != low and high < count:
            route += [(low, high), (high, low)]
    return lax.ppermute(block, axis, route)


def hop_block(moving, bit_number):
    return jax.tree.map(
        lambda part, own: part.astype(own.dtype),
        from_partner(shortened(moving), "seq", bit_number),
        moving,
    )


def on_device(
    latent, queries, key_vectors, value_vectors, proj_weight, gate_scale, text_length, split_table
):
    group_size = split_table.shape[1]
    tokens = queries.shape[0]
    feature_width = queries.shape[1]
    head_count = feature_width // HEAD_DIM
    seq_index = lax.axis_index("seq")
    item_index = seq_index // group_size
    group_place = seq_index % group_size
    counts = lax.dynamic_index_in_dim(split_table, item_index, 0, keepdims=False)
    members = jnp.arange(group_size, dtype=jnp.int32)
    offset = jnp.sum(jnp.where(members < group_place, counts, 0))
    own_count = jnp.sum(jnp.where(members == group_place, counts, 0))
    slot_index = jnp.arange(tokens, dtype=jnp.int32)
    query_live = slot_index < own_count
    text_count = jnp.sum(
        jnp.where(jnp.arange(text_length.shape[0], dtype=jnp.int32) == item_index, text_length, 0)
    )
    image_mask = query_live & (offset + slot_index >= text_count)
    query_heads = queries.reshape(tokens, head_count, HEAD_DIM)
    score_scale = 1.0 / math.sqrt(HEAD_DIM)

    def absorb(softmax_carry, stacked, key_live):
        running_max, running_sum, running_acc = softmax_carry
        length = stacked.shape[1]
        key_heads = stacked[0].reshape(length, head_count, HEAD_DIM)
        value_heads = stacked[1].reshape(length, head_count, HEAD_DIM)
        scores = (
            jnp.einsum("qhd,khd->qhk", query_heads, key_heads, preferred_element_type=jnp.float32)
            * score_scale
        )
        scores = jnp.where(key_live[None, None, :], scores, -1e30)
        new_max = jnp.maximum(running_max, jnp.max(scores, axis=2))
        shrink = jnp.exp(running_max - new_max)
        weights = jnp.exp(scores - new_max[:, :, None]) * key_live[None, None, :].astype(
            jnp.float32
        )
        running_sum = running_sum * shrink + jnp.sum(weights, axis=2)
        running_acc = running_acc * shrink[:, :, None] + jnp.einsum(
            "qhk,khd->qhd",
            weights.astype(jnp.bfloat16),
            value_heads,
            preferred_element_type=jnp.float32,
        )
        return (new_max, running_sum, running_acc)

    stacked = jnp.stack([key_vectors, value_vectors])
    softmax_carry = (
        jnp.full((tokens, head_count), -1e30, jnp.float32),
        jnp.zeros((tokens, head_count), jnp.float32),
        jnp.zeros((tokens, head_count, HEAD_DIM), jnp.float32),
    )
    softmax_carry = absorb(softmax_carry, stacked, query_live)
    if group_size > 1:
        bit_total = group_size.bit_length() - 1

        def make_branch(bit_number):

            def branch(moving):
                return hop_block(moving, bit_number)

            return branch

        branch_list = [make_branch(bit_number) for bit_number in range(bit_total)]

        def cycle_step(step_index, loop_carry):
            inner_carry, moving = loop_carry
            trailing = jnp.int32(0)
            for bit_number in range(bit_total - 1):
                trailing = trailing + (step_index % (2 << bit_number) == 0).astype(jnp.int32)
            moving = lax.switch(trailing, branch_list, moving)
            anchor = jnp.bitwise_xor(group_place, jnp.bitwise_xor(step_index, step_index // 2))
            anchor_count = jnp.sum(jnp.where(members == anchor, counts, 0))
            return (absorb(inner_carry, moving, slot_index < anchor_count), moving)

        softmax_carry, moving = lax.fori_loop(1, group_size, cycle_step, (softmax_carry, stacked))
    running_max, running_sum, running_acc = softmax_carry
    attended = (
        (running_acc / running_sum[:, :, None]).reshape(tokens, feature_width).astype(jnp.bfloat16)
    )
    row_share = tokens // lax.axis_size("tp")
    projected = lax.psum_scatter(
        jnp.dot(attended, proj_weight, preferred_element_type=jnp.float32).astype(jnp.bfloat16),
        "tp",
        scatter_dimension=0,
        tiled=True,
    ).astype(jnp.float32)
    tp_first = lax.axis_index("tp") * row_share
    my_image = lax.dynamic_slice_in_dim(image_mask, tp_first, row_share, 0)
    gate_row = lax.dynamic_index_in_dim(gate_scale, item_index, 0, keepdims=False)
    residual_base = latent.astype(jnp.float32)
    return jnp.where(
        my_image[:, None], residual_base + gate_row[None, :] * projected, residual_base
    ).astype(jnp.bfloat16)


def solution(mesh):
    in_specs = (
        P(("seq", "tp"), None),
        P("seq", "tp"),
        P("seq", "tp"),
        P("seq", "tp"),
        P("tp", None),
        P(),
        P(),
        P(),
    )
    out_specs = P(("seq", "tp"), None)

    def updated(
        latent, queries, key_vectors, value_vectors, proj_weight, gate_scale, text_length, split_table
    ):
        tokens = queries.shape[0] // mesh.shape["seq"]
        whole_request = split_table.shape[1] == 1
        text_first = mesh.shape["tp"] == 4 and tokens // 4 <= LEAST_TEXT
        return jax.shard_map(
            on_device_local if whole_request and text_first else on_device,
            mesh=mesh, in_specs=in_specs, out_specs=out_specs, check_vma=False,
        )(latent, queries, key_vectors, value_vectors, proj_weight, gate_scale, text_length, split_table)

    return updated
```

```python
import functools
import math

import jax
import jax.numpy as jnp
from jax import lax
from jax.experimental import pallas as pl
from jax.experimental.pallas import tpu as pltpu
from jax.sharding import PartitionSpec as P

HEAD_DIM = 128
LEAST_TEXT = 64
CHUNKS = 6
MESH = pl.DeviceIdType.MESH


def local_kernel(
    latent, queries, key_vectors, value_vectors, proj_weight, gate_scale, text_length, split_table,
    base, arrived,
    q_buf, k_buf, v_buf, w_buf, latent_buf, gate_buf, text_buf, table_buf,
    attended, mate_send, mate_recv, kept, far_send, near_send, near_recv, own,
    q_sem, kv_sem, w_sem, small_sem, base_sem,
    mate_sems, far_sems, near_sems,
):
    seq, tp = lax.axis_index("seq"), lax.axis_index("tp")
    core = lax.rem(tp, 2)
    mate = tp + 1 - 2 * core
    far = lax.rem(tp + 2, 4)
    far_mate = lax.rem(mate + 2, 4)
    tokens, width = q_buf.shape
    block = tokens // 4
    heads = width // HEAD_DIM
    columns = w_buf.shape[2]

    barrier = pltpu.get_barrier_semaphore()
    for other in (mate, far):
        pl.semaphore_signal(barrier, inc=1, device_id=(seq, other), device_id_type=MESH)

    q_copies = []
    for place, owner in enumerate((far_mate, far, mate, tp)):
        q_copies.append(
            pltpu.make_async_copy(
                queries.at[pl.ds(pl.multiple_of(owner * block, block), block)],
                q_buf.at[pl.ds(place * block, block)],
                q_sem.at[place],
            )
        )
    k_copy = pltpu.make_async_copy(key_vectors, k_buf, kv_sem.at[0])
    v_copy = pltpu.make_async_copy(value_vectors, v_buf, kv_sem.at[1])
    table_copy = pltpu.make_async_copy(split_table, table_buf, small_sem.at[0])
    text_copy = pltpu.make_async_copy(text_length, text_buf, small_sem.at[1])
    gate_copy = pltpu.make_async_copy(gate_scale, gate_buf, small_sem.at[2])
    latent_copy = pltpu.make_async_copy(latent, latent_buf, small_sem.at[3])
    w_copies = [
        pltpu.make_async_copy(proj_weight.at[:, pl.ds(i * columns, columns)], w_buf.at[i], w_sem.at[i])
        for i in range(CHUNKS)
    ]
    for copy in (table_copy, k_copy, *q_copies, v_copy, *w_copies, text_copy, gate_copy, latent_copy):
        copy.start()

    def remote(source, target, sems, i, other):
        return pltpu.make_async_remote_copy(
            src_ref=source.at[i],
            dst_ref=target,
            send_sem=sems.at[0, i],
            recv_sem=sems.at[1, i],
            device_id=(seq, other),
            device_id_type=MESH,
        )

    parts = [pl.ds(i * columns, columns) for i in range(CHUNKS)]
    to_mate = [remote(mate_send, mate_recv.at[i], mate_sems, i, mate) for i in range(CHUNKS)]
    to_far = [remote(far_send, arrived.at[:, parts[i]], far_sems, i, far) for i in range(CHUNKS)]
    to_owner = [remote(near_send, near_recv.at[i], near_sems, i, mate) for i in range(CHUNKS)]
    base_copies = [
        pltpu.make_async_copy(own.at[i], base.at[:, parts[i]], base_sem.at[i]) for i in range(CHUNKS)
    ]

    table_copy.wait()
    count = table_buf[seq]
    key_live = lax.broadcasted_iota(jnp.int32, (1, tokens), 1) < count
    score_scale = 1.0 / math.sqrt(HEAD_DIM)

    def attend(first):
        rows = pl.ds(first, 2 * block)
        for head in range(heads):
            part = pl.ds(head * HEAD_DIM, HEAD_DIM)
            scores = lax.dot_general(
                q_buf[rows, part], k_buf[:, part], (((1,), (1,)), ((), ())),
                preferred_element_type=jnp.float32,
            )
            scores = jnp.where(key_live, scores * score_scale, -1e30)
            top = jnp.max(scores, axis=1, keepdims=True)
            weights = jnp.exp(scores - top)
            total = jnp.sum(weights, axis=1, keepdims=True)
            summed = jnp.dot(
                weights.astype(jnp.bfloat16), v_buf[:, part], preferred_element_type=jnp.float32
            )
            attended[rows, part] = (summed / total).astype(jnp.bfloat16)

    k_copy.wait()
    for copy in q_copies:
        copy.wait()
    v_copy.wait()
    attend(0)
    text_copy.wait()
    gate_copy.wait()
    latent_copy.wait()
    text = text_buf[seq]

    def image(owner):
        position = owner * block + lax.broadcasted_iota(jnp.int32, (block, 1), 0)
        return (position >= text) & (position < count)

    far_image = image(far)
    for i in range(CHUNKS + 1):
        if i < CHUNKS:
            w_copies[i].wait()
            share = jnp.dot(
                attended[pl.ds(0, 2 * block), :], w_buf[i], preferred_element_type=jnp.float32
            )
            mate_send[i] = share[:block].astype(jnp.bfloat16)
            kept[i] = share[block:]
            if i == 0:
                pl.semaphore_wait(barrier, 2)

            @pl.when(tp != 3)
            def _():
                to_mate[i].start()

        if i >= 1:
            j = i - 1

            @pl.when(tp != 2)
            def _():
                to_mate[j].wait_recv()
                summed = kept[j] + mate_recv[j].astype(jnp.float32)
                gated = gate_buf[pl.ds(seq, 1), parts[j]] * summed
                far_send[j] = jnp.where(far_image, gated, 0.0).astype(jnp.bfloat16)
                to_far[j].start()

    attend(2 * block)
    for i in range(CHUNKS):
        share = jnp.dot(
            attended[pl.ds(2 * block, 2 * block), :], w_buf[i], preferred_element_type=jnp.float32
        )
        near_send[i] = share[:block].astype(jnp.bfloat16)
        own[i] = share[block:]

        @pl.when(tp != 1)
        def _():
            to_owner[i].start()

    near_image = image(tp)

    @pl.when(tp == 0)
    def _():
        near_recv[...] = jnp.zeros_like(near_recv)
        zero_copies = [
            pltpu.make_async_copy(near_recv.at[i], arrived.at[:, parts[i]], far_sems.at[1, i])
            for i in range(CHUNKS)
        ]
        for i in range(CHUNKS):
            zero_copies[i].start()
            own[i] = latent_buf[:, parts[i]].astype(jnp.float32)
            base_copies[i].start()
        for copy in zero_copies:
            copy.wait()

    @pl.when(tp != 0)
    def _():
        for i in range(CHUNKS):
            to_owner[i].wait_recv()
            projected = own[i] + near_recv[i].astype(jnp.float32)
            residual = latent_buf[:, parts[i]].astype(jnp.float32)
            gate = gate_buf[pl.ds(seq, 1), parts[i]]
            own[i] = jnp.where(near_image, residual + gate * projected, residual)
            base_copies[i].start()
        for i in range(CHUNKS):
            to_far[i].wait_recv()

    for copy in base_copies:
        copy.wait()
    for copies, idle in ((to_mate, 3), (to_far, 2), (to_owner, 1)):

        @pl.when(tp != idle)
        def _():
            for copy in copies:
                copy.wait_send()


def on_device_local(
    latent, queries, key_vectors, value_vectors, proj_weight, gate_scale, text_length, split_table
):
    tokens, width = queries.shape
    model = proj_weight.shape[1]
    block, columns = tokens // 4, model // CHUNKS
    in_hbm = pl.BlockSpec(memory_space=pltpu.HBM)
    blocks16 = pltpu.VMEM((CHUNKS, block, columns), jnp.bfloat16)
    blocks32 = pltpu.VMEM((CHUNKS, block, columns), jnp.float32)
    base, arrived = pl.pallas_call(
        local_kernel,
        out_shape=(
            jax.ShapeDtypeStruct(latent.shape, jnp.float32),
            jax.ShapeDtypeStruct(latent.shape, jnp.bfloat16),
        ),
        in_specs=[in_hbm] * 8,
        out_specs=(in_hbm, in_hbm),
        scratch_shapes=[
            pltpu.VMEM((tokens, width), jnp.bfloat16),
            pltpu.VMEM((tokens, width), jnp.bfloat16),
            pltpu.VMEM((tokens, width), jnp.bfloat16),
            pltpu.VMEM((CHUNKS, width, columns), jnp.bfloat16),
            pltpu.VMEM(latent.shape, jnp.bfloat16),
            pltpu.VMEM(gate_scale.shape, jnp.float32),
            pltpu.SMEM(text_length.shape, jnp.int32),
            pltpu.SMEM((split_table.size,), jnp.int32),
            pltpu.VMEM((tokens, width), jnp.bfloat16),
            blocks16, blocks16, blocks32, blocks16, blocks16, blocks16, blocks32,
            pltpu.SemaphoreType.DMA((4,)),
            pltpu.SemaphoreType.DMA((2,)),
            pltpu.SemaphoreType.DMA((CHUNKS,)),
            pltpu.SemaphoreType.DMA((4,)),
            pltpu.SemaphoreType.DMA((CHUNKS,)),
            pltpu.SemaphoreType.DMA((2, CHUNKS)),
            pltpu.SemaphoreType.DMA((2, CHUNKS)),
            pltpu.SemaphoreType.DMA((2, CHUNKS)),
        ],
        compiler_params=pltpu.CompilerParams(
            collective_id=0, has_side_effects=True, vmem_limit_bytes=64 * 2**20
        ),
        cost_estimate=pl.CostEstimate(
            flops=2 * tokens * width * (model + 2 * tokens), bytes_accessed=4 * 2**20, transcendentals=0
        ),
    )(latent, queries, key_vectors, value_vectors, proj_weight, gate_scale, text_length, split_table.reshape(-1))
    return (base + arrived.astype(jnp.float32)).astype(jnp.bfloat16)


def shortened(shard):
    return jax.tree.map(lambda a: a.astype(jnp.bfloat16) if a.dtype == jnp.float32 else a, shard)


def from_partner(block, axis, stride):
    count = lax.axis_size(axis)
    route = []
    for low in range(count):
        high = low | 1 << stride
        if high != low and high < count:
            route += [(low, high), (high, low)]
    return lax.ppermute(block, axis, route)


def hop_block(moving, bit_number):
    return jax.tree.map(
        lambda part, own: part.astype(own.dtype),
        from_partner(shortened(moving), "seq", bit_number),
        moving,
    )


def on_device(
    latent, queries, key_vectors, value_vectors, proj_weight, gate_scale, text_length, split_table
):
    group_size = split_table.shape[1]
    tokens = queries.shape[0]
    feature_width = queries.shape[1]
    head_count = feature_width // HEAD_DIM
    seq_index = lax.axis_index("seq")
    item_index = seq_index // group_size
    group_place = seq_index % group_size
    counts = lax.dynamic_index_in_dim(split_table, item_index, 0, keepdims=False)
    members = jnp.arange(group_size, dtype=jnp.int32)
    offset = jnp.sum(jnp.where(members < group_place, counts, 0))
    own_count = jnp.sum(jnp.where(members == group_place, counts, 0))
    slot_index = jnp.arange(tokens, dtype=jnp.int32)
    query_live = slot_index < own_count
    text_count = jnp.sum(
        jnp.where(jnp.arange(text_length.shape[0], dtype=jnp.int32) == item_index, text_length, 0)
    )
    image_mask = query_live & (offset + slot_index >= text_count)
    query_heads = queries.reshape(tokens, head_count, HEAD_DIM)
    score_scale = 1.0 / math.sqrt(HEAD_DIM)

    def absorb(softmax_carry, stacked, key_live):
        running_max, running_sum, running_acc = softmax_carry
        length = stacked.shape[1]
        key_heads = stacked[0].reshape(length, head_count, HEAD_DIM)
        value_heads = stacked[1].reshape(length, head_count, HEAD_DIM)
        scores = (
            jnp.einsum("qhd,khd->qhk", query_heads, key_heads, preferred_element_type=jnp.float32)
            * score_scale
        )
        scores = jnp.where(key_live[None, None, :], scores, -1e30)
        new_max = jnp.maximum(running_max, jnp.max(scores, axis=2))
        shrink = jnp.exp(running_max - new_max)
        weights = jnp.exp(scores - new_max[:, :, None]) * key_live[None, None, :].astype(
            jnp.float32
        )
        running_sum = running_sum * shrink + jnp.sum(weights, axis=2)
        running_acc = running_acc * shrink[:, :, None] + jnp.einsum(
            "qhk,khd->qhd",
            weights.astype(jnp.bfloat16),
            value_heads,
            preferred_element_type=jnp.float32,
        )
        return (new_max, running_sum, running_acc)

    stacked = jnp.stack([key_vectors, value_vectors])
    softmax_carry = (
        jnp.full((tokens, head_count), -1e30, jnp.float32),
        jnp.zeros((tokens, head_count), jnp.float32),
        jnp.zeros((tokens, head_count, HEAD_DIM), jnp.float32),
    )
    softmax_carry = absorb(softmax_carry, stacked, query_live)
    if group_size > 1:
        bit_total = group_size.bit_length() - 1

        def make_branch(bit_number):

            def branch(moving):
                return hop_block(moving, bit_number)

            return branch

        branch_list = [make_branch(bit_number) for bit_number in range(bit_total)]

        def cycle_step(step_index, loop_carry):
            inner_carry, moving = loop_carry
            trailing = jnp.int32(0)
            for bit_number in range(bit_total - 1):
                trailing = trailing + (step_index % (2 << bit_number) == 0).astype(jnp.int32)
            moving = lax.switch(trailing, branch_list, moving)
            anchor = jnp.bitwise_xor(group_place, jnp.bitwise_xor(step_index, step_index // 2))
            anchor_count = jnp.sum(jnp.where(members == anchor, counts, 0))
            return (absorb(inner_carry, moving, slot_index < anchor_count), moving)

        softmax_carry, moving = lax.fori_loop(1, group_size, cycle_step, (softmax_carry, stacked))
    running_max, running_sum, running_acc = softmax_carry
    attended = (
        (running_acc / running_sum[:, :, None]).reshape(tokens, feature_width).astype(jnp.bfloat16)
    )
    row_share = tokens // lax.axis_size("tp")
    projected = lax.psum_scatter(
        jnp.dot(attended, proj_weight, preferred_element_type=jnp.float32).astype(jnp.bfloat16),
        "tp",
        scatter_dimension=0,
        tiled=True,
    ).astype(jnp.float32)
    tp_first = lax.axis_index("tp") * row_share
    my_image = lax.dynamic_slice_in_dim(image_mask, tp_first, row_share, 0)
    gate_row = lax.dynamic_index_in_dim(gate_scale, item_index, 0, keepdims=False)
    residual_base = latent.astype(jnp.float32)
    return jnp.where(
        my_image[:, None], residual_base + gate_row[None, :] * projected, residual_base
    ).astype(jnp.bfloat16)


def solution(mesh):
    in_specs = (
        P(("seq", "tp"), None),
        P("seq", "tp"),
        P("seq", "tp"),
        P("seq", "tp"),
        P("tp", None),
        P(),
        P(),
        P(),
    )
    out_specs = P(("seq", "tp"), None)

    def updated(
        latent, queries, key_vectors, value_vectors, proj_weight, gate_scale, text_length, split_table
    ):
        tokens = queries.shape[0] // mesh.shape["seq"]
        whole_request = split_table.shape[1] == 1
        text_first = mesh.shape["tp"] == 4 and tokens // 4 <= LEAST_TEXT
        return jax.shard_map(
            on_device_local if whole_request and text_first else on_device,
            mesh=mesh, in_specs=in_specs, out_specs=out_specs, check_vma=False,
        )(latent, queries, key_vectors, value_vectors, proj_weight, gate_scale, text_length, split_table)

    return updated
```

```python
import functools
import math

import jax
import jax.numpy as jnp
from jax import lax
from jax.experimental import pallas as pl
from jax.experimental.pallas import tpu as pltpu
from jax.sharding import PartitionSpec as P

HEAD_DIM = 128
LEAST_TEXT = 64
CHUNKS = 12
AHEAD = 4
MESH = pl.DeviceIdType.MESH


def local_kernel(
    latent, queries, key_vectors, value_vectors, proj_weight, gate_scale, text_length, split_table,
    base, arrived,
    q_buf, k_buf, v_buf, w_buf, latent_buf, gate_buf, text_buf, table_buf,
    attended, mate_send, mate_recv, kept, far_send, near_send, near_recv, own,
    q_sem, kv_sem, w_sem, small_sem, base_sem,
    mate_sems, far_sems, near_sems,
):
    seq, tp = lax.axis_index("seq"), lax.axis_index("tp")
    core = lax.rem(tp, 2)
    mate = tp + 1 - 2 * core
    far = lax.rem(tp + 2, 4)
    far_mate = lax.rem(mate + 2, 4)
    tokens, width = q_buf.shape
    block = tokens // 4
    heads = width // HEAD_DIM
    columns = w_buf.shape[2]

    barrier = pltpu.get_barrier_semaphore()
    for other in (mate, far):
        pl.semaphore_signal(barrier, inc=1, device_id=(seq, other), device_id_type=MESH)

    q_copies = []
    for place, owner in enumerate((far_mate, far, mate, tp)):
        q_copies.append(
            pltpu.make_async_copy(
                queries.at[pl.ds(pl.multiple_of(owner * block, block), block)],
                q_buf.at[pl.ds(place * block, block)],
                q_sem.at[place],
            )
        )
    k_copy = pltpu.make_async_copy(key_vectors, k_buf, kv_sem.at[0])
    v_copies = [
        pltpu.make_async_copy(
            value_vectors.at[:, pl.ds(head * HEAD_DIM, HEAD_DIM)],
            v_buf.at[:, pl.ds(2 * head * HEAD_DIM, HEAD_DIM)],
            kv_sem.at[1 + head],
        )
        for head in range(heads)
    ]
    table_copy = pltpu.make_async_copy(split_table, table_buf, small_sem.at[0])
    text_copy = pltpu.make_async_copy(text_length, text_buf, small_sem.at[1])
    gate_copy = pltpu.make_async_copy(gate_scale, gate_buf, small_sem.at[2])
    latent_copy = pltpu.make_async_copy(latent, latent_buf, small_sem.at[3])
    w_copies = [
        pltpu.make_async_copy(proj_weight.at[:, pl.ds(i * columns, columns)], w_buf.at[i], w_sem.at[i])
        for i in range(CHUNKS)
    ]
    for copy in (table_copy, k_copy, *q_copies, *v_copies, *w_copies, text_copy, gate_copy, latent_copy):
        copy.start()

    def remote(source, target, sems, i, other):
        return pltpu.make_async_remote_copy(
            src_ref=source.at[i],
            dst_ref=target,
            send_sem=sems.at[0, i],
            recv_sem=sems.at[1, i],
            device_id=(seq, other),
            device_id_type=MESH,
        )

    parts = [pl.ds(i * columns, columns) for i in range(CHUNKS)]
    to_mate = [remote(mate_send, mate_recv.at[i], mate_sems, i, mate) for i in range(CHUNKS)]
    to_far = [remote(far_send, arrived.at[:, parts[i]], far_sems, i, far) for i in range(CHUNKS)]
    to_owner = [remote(near_send, near_recv.at[i], near_sems, i, mate) for i in range(CHUNKS)]
    base_copies = [
        pltpu.make_async_copy(own.at[i], base.at[:, parts[i]], base_sem.at[i]) for i in range(CHUNKS)
    ]

    for head in range(heads):
        v_buf[:, pl.ds((2 * head + 1) * HEAD_DIM, HEAD_DIM)] = jnp.ones((tokens, HEAD_DIM), jnp.bfloat16)

    table_copy.wait()
    count = table_buf[seq]
    key_live = lax.broadcasted_iota(jnp.int32, (1, tokens), 1) < count
    score_scale = math.log2(math.e) / math.sqrt(HEAD_DIM)

    def attend(first):
        rows = pl.ds(first, 2 * block)
        columns_of = [pl.ds(head * HEAD_DIM, HEAD_DIM) for head in range(heads)]
        scores = [
            lax.dot_general(
                q_buf[rows, part], k_buf[:, part], (((1,), (1,)), ((), ())),
                preferred_element_type=jnp.float32,
            )
            for part in columns_of
        ]
        scores = [jnp.where(key_live, one * score_scale, -1e30) for one in scores]
        weights = [jnp.exp2(one - jnp.max(one, axis=1, keepdims=True)) for one in scores]
        summed = [
            jnp.dot(
                one.astype(jnp.bfloat16), v_buf[:, pl.ds(2 * head * HEAD_DIM, 2 * HEAD_DIM)],
                preferred_element_type=jnp.float32,
            )
            for head, one in enumerate(weights)
        ]
        for part, one in zip(columns_of, summed):
            attended[rows, part] = (one[:, :HEAD_DIM] / one[:, HEAD_DIM:]).astype(jnp.bfloat16)

    k_copy.wait()
    for copy in q_copies:
        copy.wait()
    for copy in v_copies:
        copy.wait()
    attend(0)
    text_copy.wait()
    gate_copy.wait()
    latent_copy.wait()
    text = text_buf[seq]

    def image(owner):
        position = owner * block + lax.broadcasted_iota(jnp.int32, (block, 1), 0)
        return (position >= text) & (position < count)

    far_image = image(far)
    for i in range(CHUNKS + AHEAD):
        if i < CHUNKS:
            w_copies[i].wait()
            share = jnp.dot(
                attended[pl.ds(0, 2 * block), :], w_buf[i], preferred_element_type=jnp.float32
            )
            mate_send[i] = share[:block].astype(jnp.bfloat16)
            kept[i] = share[block:]
            if i == 0:
                pl.semaphore_wait(barrier, 2)

            @pl.when(tp != 3)
            def _():
                to_mate[i].start()

        if i >= AHEAD:
            j = i - AHEAD

            @pl.when(tp != 2)
            def _():
                to_mate[j].wait_recv()
                summed = kept[j] + mate_recv[j].astype(jnp.float32)
                gated = gate_buf[pl.ds(seq, 1), parts[j]] * summed
                far_send[j] = jnp.where(far_image, gated, 0.0).astype(jnp.bfloat16)
                to_far[j].start()

    attend(2 * block)
    for i in range(CHUNKS):
        share = jnp.dot(
            attended[pl.ds(2 * block, 2 * block), :], w_buf[i], preferred_element_type=jnp.float32
        )
        near_send[i] = share[:block].astype(jnp.bfloat16)
        own[i] = share[block:]

        @pl.when(tp != 1)
        def _():
            to_owner[i].start()

    near_image = image(tp)

    @pl.when(tp == 0)
    def _():
        near_recv[...] = jnp.zeros_like(near_recv)
        zero_copies = [
            pltpu.make_async_copy(near_recv.at[i], arrived.at[:, parts[i]], far_sems.at[1, i])
            for i in range(CHUNKS)
        ]
        for i in range(CHUNKS):
            zero_copies[i].start()
            own[i] = latent_buf[:, parts[i]].astype(jnp.float32)
            base_copies[i].start()
        for copy in zero_copies:
            copy.wait()

    @pl.when(tp != 0)
    def _():
        for i in range(CHUNKS):
            to_owner[i].wait_recv()
            projected = own[i] + near_recv[i].astype(jnp.float32)
            residual = latent_buf[:, parts[i]].astype(jnp.float32)
            gate = gate_buf[pl.ds(seq, 1), parts[i]]
            own[i] = jnp.where(near_image, residual + gate * projected, residual)
            base_copies[i].start()
        for i in range(CHUNKS):
            to_far[i].wait_recv()

    for copy in base_copies:
        copy.wait()
    for copies, idle in ((to_mate, 3), (to_far, 2), (to_owner, 1)):

        @pl.when(tp != idle)
        def _():
            for copy in copies:
                copy.wait_send()


def on_device_local(
    latent, queries, key_vectors, value_vectors, proj_weight, gate_scale, text_length, split_table
):
    tokens, width = queries.shape
    model = proj_weight.shape[1]
    block, columns = tokens // 4, model // CHUNKS
    in_hbm = pl.BlockSpec(memory_space=pltpu.HBM)
    blocks16 = pltpu.VMEM((CHUNKS, block, columns), jnp.bfloat16)
    blocks32 = pltpu.VMEM((CHUNKS, block, columns), jnp.float32)
    base, arrived = pl.pallas_call(
        local_kernel,
        out_shape=(
            jax.ShapeDtypeStruct(latent.shape, jnp.float32),
            jax.ShapeDtypeStruct(latent.shape, jnp.bfloat16),
        ),
        in_specs=[in_hbm] * 8,
        out_specs=(in_hbm, in_hbm),
        scratch_shapes=[
            pltpu.VMEM((tokens, width), jnp.bfloat16),
            pltpu.VMEM((tokens, width), jnp.bfloat16),
            pltpu.VMEM((tokens, 2 * width), jnp.bfloat16),
            pltpu.VMEM((CHUNKS, width, columns), jnp.bfloat16),
            pltpu.VMEM(latent.shape, jnp.bfloat16),
            pltpu.VMEM(gate_scale.shape, jnp.float32),
            pltpu.SMEM(text_length.shape, jnp.int32),
            pltpu.SMEM((split_table.size,), jnp.int32),
            pltpu.VMEM((tokens, width), jnp.bfloat16),
            blocks16, blocks16, blocks32, blocks16, blocks16, blocks16, blocks32,
            pltpu.SemaphoreType.DMA((4,)),
            pltpu.SemaphoreType.DMA((1 + width // HEAD_DIM,)),
            pltpu.SemaphoreType.DMA((CHUNKS,)),
            pltpu.SemaphoreType.DMA((4,)),
            pltpu.SemaphoreType.DMA((CHUNKS,)),
            pltpu.SemaphoreType.DMA((2, CHUNKS)),
            pltpu.SemaphoreType.DMA((2, CHUNKS)),
            pltpu.SemaphoreType.DMA((2, CHUNKS)),
        ],
        compiler_params=pltpu.CompilerParams(
            collective_id=0, has_side_effects=True, vmem_limit_bytes=64 * 2**20
        ),
        cost_estimate=pl.CostEstimate(
            flops=2 * tokens * width * (model + 2 * tokens), bytes_accessed=4 * 2**20, transcendentals=0
        ),
    )(latent, queries, key_vectors, value_vectors, proj_weight, gate_scale, text_length, split_table.reshape(-1))
    return (base + arrived.astype(jnp.float32)).astype(jnp.bfloat16)


def shortened(shard):
    return jax.tree.map(lambda a: a.astype(jnp.bfloat16) if a.dtype == jnp.float32 else a, shard)


def from_partner(block, axis, stride):
    count = lax.axis_size(axis)
    route = []
    for low in range(count):
        high = low | 1 << stride
        if high != low and high < count:
            route += [(low, high), (high, low)]
    return lax.ppermute(block, axis, route)


def hop_block(moving, bit_number):
    return jax.tree.map(
        lambda part, own: part.astype(own.dtype),
        from_partner(shortened(moving), "seq", bit_number),
        moving,
    )


def on_device(
    latent, queries, key_vectors, value_vectors, proj_weight, gate_scale, text_length, split_table
):
    group_size = split_table.shape[1]
    tokens = queries.shape[0]
    feature_width = queries.shape[1]
    head_count = feature_width // HEAD_DIM
    seq_index = lax.axis_index("seq")
    item_index = seq_index // group_size
    group_place = seq_index % group_size
    counts = lax.dynamic_index_in_dim(split_table, item_index, 0, keepdims=False)
    members = jnp.arange(group_size, dtype=jnp.int32)
    offset = jnp.sum(jnp.where(members < group_place, counts, 0))
    own_count = jnp.sum(jnp.where(members == group_place, counts, 0))
    slot_index = jnp.arange(tokens, dtype=jnp.int32)
    query_live = slot_index < own_count
    text_count = jnp.sum(
        jnp.where(jnp.arange(text_length.shape[0], dtype=jnp.int32) == item_index, text_length, 0)
    )
    image_mask = query_live & (offset + slot_index >= text_count)
    query_heads = queries.reshape(tokens, head_count, HEAD_DIM)
    score_scale = 1.0 / math.sqrt(HEAD_DIM)

    def absorb(softmax_carry, stacked, key_live):
        running_max, running_sum, running_acc = softmax_carry
        length = stacked.shape[1]
        key_heads = stacked[0].reshape(length, head_count, HEAD_DIM)
        value_heads = stacked[1].reshape(length, head_count, HEAD_DIM)
        scores = (
            jnp.einsum("qhd,khd->qhk", query_heads, key_heads, preferred_element_type=jnp.float32)
            * score_scale
        )
        scores = jnp.where(key_live[None, None, :], scores, -1e30)
        new_max = jnp.maximum(running_max, jnp.max(scores, axis=2))
        shrink = jnp.exp(running_max - new_max)
        weights = jnp.exp(scores - new_max[:, :, None]) * key_live[None, None, :].astype(
            jnp.float32
        )
        running_sum = running_sum * shrink + jnp.sum(weights, axis=2)
        running_acc = running_acc * shrink[:, :, None] + jnp.einsum(
            "qhk,khd->qhd",
            weights.astype(jnp.bfloat16),
            value_heads,
            preferred_element_type=jnp.float32,
        )
        return (new_max, running_sum, running_acc)

    stacked = jnp.stack([key_vectors, value_vectors])
    softmax_carry = (
        jnp.full((tokens, head_count), -1e30, jnp.float32),
        jnp.zeros((tokens, head_count), jnp.float32),
        jnp.zeros((tokens, head_count, HEAD_DIM), jnp.float32),
    )
    softmax_carry = absorb(softmax_carry, stacked, query_live)
    if group_size > 1:
        bit_total = group_size.bit_length() - 1

        def make_branch(bit_number):

            def branch(moving):
                return hop_block(moving, bit_number)

            return branch

        branch_list = [make_branch(bit_number) for bit_number in range(bit_total)]

        def cycle_step(step_index, loop_carry):
            inner_carry, moving = loop_carry
            trailing = jnp.int32(0)
            for bit_number in range(bit_total - 1):
                trailing = trailing + (step_index % (2 << bit_number) == 0).astype(jnp.int32)
            moving = lax.switch(trailing, branch_list, moving)
            anchor = jnp.bitwise_xor(group_place, jnp.bitwise_xor(step_index, step_index // 2))
            anchor_count = jnp.sum(jnp.where(members == anchor, counts, 0))
            return (absorb(inner_carry, moving, slot_index < anchor_count), moving)

        softmax_carry, moving = lax.fori_loop(1, group_size, cycle_step, (softmax_carry, stacked))
    running_max, running_sum, running_acc = softmax_carry
    attended = (
        (running_acc / running_sum[:, :, None]).reshape(tokens, feature_width).astype(jnp.bfloat16)
    )
    row_share = tokens // lax.axis_size("tp")
    projected = lax.psum_scatter(
        jnp.dot(attended, proj_weight, preferred_element_type=jnp.float32).astype(jnp.bfloat16),
        "tp",
        scatter_dimension=0,
        tiled=True,
    ).astype(jnp.float32)
    tp_first = lax.axis_index("tp") * row_share
    my_image = lax.dynamic_slice_in_dim(image_mask, tp_first, row_share, 0)
    gate_row = lax.dynamic_index_in_dim(gate_scale, item_index, 0, keepdims=False)
    residual_base = latent.astype(jnp.float32)
    return jnp.where(
        my_image[:, None], residual_base + gate_row[None, :] * projected, residual_base
    ).astype(jnp.bfloat16)


def solution(mesh):
    in_specs = (
        P(("seq", "tp"), None),
        P("seq", "tp"),
        P("seq", "tp"),
        P("seq", "tp"),
        P("tp", None),
        P(),
        P(),
        P(),
    )
    out_specs = P(("seq", "tp"), None)

    def updated(
        latent, queries, key_vectors, value_vectors, proj_weight, gate_scale, text_length, split_table
    ):
        tokens = queries.shape[0] // mesh.shape["seq"]
        whole_request = split_table.shape[1] == 1
        text_first = mesh.shape["tp"] == 4 and tokens // 4 <= LEAST_TEXT
        return jax.shard_map(
            on_device_local if whole_request and text_first else on_device,
            mesh=mesh, in_specs=in_specs, out_specs=out_specs, check_vma=False,
        )(latent, queries, key_vectors, value_vectors, proj_weight, gate_scale, text_length, split_table)

    return updated
```

```python
import functools
import math

import jax
import jax.numpy as jnp
from jax import lax
from jax.experimental import pallas as pl
from jax.experimental.pallas import tpu as pltpu
from jax.sharding import PartitionSpec as P

HEAD_DIM = 128
LEAST_TEXT = 64
CHUNKS = 12
AHEAD = 3
MESH = pl.DeviceIdType.MESH


def local_kernel(
    latent, queries, key_vectors, value_vectors, proj_weight, gate_scale, text_length, split_table,
    base, arrived,
    q_buf, k_buf, v_buf, w_buf, latent_buf, gate_buf, text_buf, table_buf,
    attended, mate_send, mate_recv, kept, far_send, near_send, near_recv, own,
    q_sem, kv_sem, w_sem, small_sem, base_sem,
    mate_sems, far_sems, near_sems,
):
    seq, tp = lax.axis_index("seq"), lax.axis_index("tp")
    core = lax.rem(tp, 2)
    mate = tp + 1 - 2 * core
    far = lax.rem(tp + 2, 4)
    far_mate = lax.rem(mate + 2, 4)
    tokens, width = q_buf.shape
    block = tokens // 4
    heads = width // HEAD_DIM
    columns = w_buf.shape[2]

    barrier = pltpu.get_barrier_semaphore()
    for other in (mate, far):
        pl.semaphore_signal(barrier, inc=1, device_id=(seq, other), device_id_type=MESH)

    q_copies = []
    for place, owner in enumerate((far_mate, far, mate, tp)):
        q_copies.append(
            pltpu.make_async_copy(
                queries.at[pl.ds(pl.multiple_of(owner * block, block), block)],
                q_buf.at[pl.ds(place * block, block)],
                q_sem.at[place],
            )
        )
    k_copy = pltpu.make_async_copy(key_vectors, k_buf, kv_sem.at[0])
    v_copies = [
        pltpu.make_async_copy(
            value_vectors.at[:, pl.ds(head * HEAD_DIM, HEAD_DIM)],
            v_buf.at[:, pl.ds(2 * head * HEAD_DIM, HEAD_DIM)],
            kv_sem.at[1 + head],
        )
        for head in range(heads)
    ]
    table_copy = pltpu.make_async_copy(split_table, table_buf, small_sem.at[0])
    text_copy = pltpu.make_async_copy(text_length, text_buf, small_sem.at[1])
    gate_copy = pltpu.make_async_copy(gate_scale, gate_buf, small_sem.at[2])
    latent_copy = pltpu.make_async_copy(latent, latent_buf, small_sem.at[3])
    w_copies = [
        pltpu.make_async_copy(proj_weight.at[:, pl.ds(i * columns, columns)], w_buf.at[i], w_sem.at[i])
        for i in range(CHUNKS)
    ]
    for copy in (table_copy, k_copy, *q_copies, *v_copies, *w_copies, text_copy, gate_copy, latent_copy):
        copy.start()

    def remote(source, target, sems, i, other):
        return pltpu.make_async_remote_copy(
            src_ref=source.at[i],
            dst_ref=target,
            send_sem=sems.at[0, i],
            recv_sem=sems.at[1, i],
            device_id=(seq, other),
            device_id_type=MESH,
        )

    parts = [pl.ds(i * columns, columns) for i in range(CHUNKS)]
    to_mate = [remote(mate_send, mate_recv.at[i], mate_sems, i, mate) for i in range(CHUNKS)]
    to_far = [remote(far_send, arrived.at[:, parts[i]], far_sems, i, far) for i in range(CHUNKS)]
    to_owner = [remote(near_send, near_recv.at[i], near_sems, i, mate) for i in range(CHUNKS)]
    base_copies = [
        pltpu.make_async_copy(own.at[i], base.at[:, parts[i]], base_sem.at[i]) for i in range(CHUNKS)
    ]

    for head in range(heads):
        v_buf[:, pl.ds((2 * head + 1) * HEAD_DIM, HEAD_DIM)] = jnp.ones((tokens, HEAD_DIM), jnp.bfloat16)

    table_copy.wait()
    count = table_buf[seq]
    key_live = lax.broadcasted_iota(jnp.int32, (1, tokens), 1) < count
    score_scale = math.log2(math.e) / math.sqrt(HEAD_DIM)

    def attend(first, length):
        rows = pl.ds(first, length)
        columns_of = [pl.ds(head * HEAD_DIM, HEAD_DIM) for head in range(heads)]
        scores = [
            lax.dot_general(
                q_buf[rows, part], k_buf[:, part], (((1,), (1,)), ((), ())),
                preferred_element_type=jnp.float32,
            )
            for part in columns_of
        ]
        scores = [jnp.where(key_live, one * score_scale, -1e30) for one in scores]
        weights = [jnp.exp2(one - jnp.max(one, axis=1, keepdims=True)) for one in scores]
        summed = [
            jnp.dot(
                one.astype(jnp.bfloat16), v_buf[:, pl.ds(2 * head * HEAD_DIM, 2 * HEAD_DIM)],
                preferred_element_type=jnp.float32,
            )
            for head, one in enumerate(weights)
        ]
        for part, one in zip(columns_of, summed):
            attended[rows, part] = (one[:, :HEAD_DIM] / one[:, HEAD_DIM:]).astype(jnp.bfloat16)

    k_copy.wait()
    for copy in q_copies:
        copy.wait()
    for copy in v_copies:
        copy.wait()
    def send_to_mate(i, share):
        mate_send[i] = share.astype(jnp.bfloat16)

        @pl.when(tp != 3)
        def _():
            to_mate[i].start()

    def product(first, length, i):
        return jnp.dot(
            attended[pl.ds(first, length), :], w_buf[i], preferred_element_type=jnp.float32
        )

    attend(0, block)
    pl.semaphore_wait(barrier, 2)
    for i in range(AHEAD):
        w_copies[i].wait()
        send_to_mate(i, product(0, block, i))
    attend(block, block)

    text_copy.wait()
    gate_copy.wait()
    latent_copy.wait()
    text = text_buf[seq]

    def image(owner):
        position = owner * block + lax.broadcasted_iota(jnp.int32, (block, 1), 0)
        return (position >= text) & (position < count)

    far_image = image(far)
    for i in range(CHUNKS):
        if i < AHEAD:
            kept[i] = product(block, block, i)

        @pl.when(tp != 2)
        def _():
            to_mate[i].wait_recv()
            summed = kept[i] + mate_recv[i].astype(jnp.float32)
            gated = gate_buf[pl.ds(seq, 1), parts[i]] * summed
            far_send[i] = jnp.where(far_image, gated, 0.0).astype(jnp.bfloat16)
            to_far[i].start()

        later = i + AHEAD
        if later < CHUNKS:
            w_copies[later].wait()
            share = product(0, 2 * block, later)
            kept[later] = share[block:]
            send_to_mate(later, share[:block])

    attend(2 * block, 2 * block)
    for i in range(CHUNKS):
        share = jnp.dot(
            attended[pl.ds(2 * block, 2 * block), :], w_buf[i], preferred_element_type=jnp.float32
        )
        near_send[i] = share[:block].astype(jnp.bfloat16)
        own[i] = share[block:]

        @pl.when(tp != 1)
        def _():
            to_owner[i].start()

    near_image = image(tp)

    @pl.when(tp == 0)
    def _():
        near_recv[...] = jnp.zeros_like(near_recv)
        zero_copies = [
            pltpu.make_async_copy(near_recv.at[i], arrived.at[:, parts[i]], far_sems.at[1, i])
            for i in range(CHUNKS)
        ]
        for i in range(CHUNKS):
            zero_copies[i].start()
            own[i] = latent_buf[:, parts[i]].astype(jnp.float32)
            base_copies[i].start()
        for copy in zero_copies:
            copy.wait()

    @pl.when(tp != 0)
    def _():
        for i in range(CHUNKS):
            to_owner[i].wait_recv()
            projected = own[i] + near_recv[i].astype(jnp.float32)
            residual = latent_buf[:, parts[i]].astype(jnp.float32)
            gate = gate_buf[pl.ds(seq, 1), parts[i]]
            own[i] = jnp.where(near_image, residual + gate * projected, residual)
            base_copies[i].start()
        for i in range(CHUNKS):
            to_far[i].wait_recv()

    for copy in base_copies:
        copy.wait()
    for copies, idle in ((to_mate, 3), (to_far, 2), (to_owner, 1)):

        @pl.when(tp != idle)
        def _():
            for copy in copies:
                copy.wait_send()


def on_device_local(
    latent, queries, key_vectors, value_vectors, proj_weight, gate_scale, text_length, split_table
):
    tokens, width = queries.shape
    model = proj_weight.shape[1]
    block, columns = tokens // 4, model // CHUNKS
    in_hbm = pl.BlockSpec(memory_space=pltpu.HBM)
    blocks16 = pltpu.VMEM((CHUNKS, block, columns), jnp.bfloat16)
    blocks32 = pltpu.VMEM((CHUNKS, block, columns), jnp.float32)
    base, arrived = pl.pallas_call(
        local_kernel,
        out_shape=(
            jax.ShapeDtypeStruct(latent.shape, jnp.float32),
            jax.ShapeDtypeStruct(latent.shape, jnp.bfloat16),
        ),
        in_specs=[in_hbm] * 8,
        out_specs=(in_hbm, in_hbm),
        scratch_shapes=[
            pltpu.VMEM((tokens, width), jnp.bfloat16),
            pltpu.VMEM((tokens, width), jnp.bfloat16),
            pltpu.VMEM((tokens, 2 * width), jnp.bfloat16),
            pltpu.VMEM((CHUNKS, width, columns), jnp.bfloat16),
            pltpu.VMEM(latent.shape, jnp.bfloat16),
            pltpu.VMEM(gate_scale.shape, jnp.float32),
            pltpu.SMEM(text_length.shape, jnp.int32),
            pltpu.SMEM((split_table.size,), jnp.int32),
            pltpu.VMEM((tokens, width), jnp.bfloat16),
            blocks16, blocks16, blocks32, blocks16, blocks16, blocks16, blocks32,
            pltpu.SemaphoreType.DMA((4,)),
            pltpu.SemaphoreType.DMA((1 + width // HEAD_DIM,)),
            pltpu.SemaphoreType.DMA((CHUNKS,)),
            pltpu.SemaphoreType.DMA((4,)),
            pltpu.SemaphoreType.DMA((CHUNKS,)),
            pltpu.SemaphoreType.DMA((2, CHUNKS)),
            pltpu.SemaphoreType.DMA((2, CHUNKS)),
            pltpu.SemaphoreType.DMA((2, CHUNKS)),
        ],
        compiler_params=pltpu.CompilerParams(
            collective_id=0, has_side_effects=True, vmem_limit_bytes=64 * 2**20
        ),
        cost_estimate=pl.CostEstimate(
            flops=2 * tokens * width * (model + 2 * tokens), bytes_accessed=4 * 2**20, transcendentals=0
        ),
    )(latent, queries, key_vectors, value_vectors, proj_weight, gate_scale, text_length, split_table.reshape(-1))
    return (base + arrived.astype(jnp.float32)).astype(jnp.bfloat16)


def shortened(shard):
    return jax.tree.map(lambda a: a.astype(jnp.bfloat16) if a.dtype == jnp.float32 else a, shard)


def from_partner(block, axis, stride):
    count = lax.axis_size(axis)
    route = []
    for low in range(count):
        high = low | 1 << stride
        if high != low and high < count:
            route += [(low, high), (high, low)]
    return lax.ppermute(block, axis, route)


def hop_block(moving, bit_number):
    return jax.tree.map(
        lambda part, own: part.astype(own.dtype),
        from_partner(shortened(moving), "seq", bit_number),
        moving,
    )


def on_device(
    latent, queries, key_vectors, value_vectors, proj_weight, gate_scale, text_length, split_table
):
    group_size = split_table.shape[1]
    tokens = queries.shape[0]
    feature_width = queries.shape[1]
    head_count = feature_width // HEAD_DIM
    seq_index = lax.axis_index("seq")
    item_index = seq_index // group_size
    group_place = seq_index % group_size
    counts = lax.dynamic_index_in_dim(split_table, item_index, 0, keepdims=False)
    members = jnp.arange(group_size, dtype=jnp.int32)
    offset = jnp.sum(jnp.where(members < group_place, counts, 0))
    own_count = jnp.sum(jnp.where(members == group_place, counts, 0))
    slot_index = jnp.arange(tokens, dtype=jnp.int32)
    query_live = slot_index < own_count
    text_count = jnp.sum(
        jnp.where(jnp.arange(text_length.shape[0], dtype=jnp.int32) == item_index, text_length, 0)
    )
    image_mask = query_live & (offset + slot_index >= text_count)
    query_heads = queries.reshape(tokens, head_count, HEAD_DIM)
    score_scale = 1.0 / math.sqrt(HEAD_DIM)

    def absorb(softmax_carry, stacked, key_live):
        running_max, running_sum, running_acc = softmax_carry
        length = stacked.shape[1]
        key_heads = stacked[0].reshape(length, head_count, HEAD_DIM)
        value_heads = stacked[1].reshape(length, head_count, HEAD_DIM)
        scores = (
            jnp.einsum("qhd,khd->qhk", query_heads, key_heads, preferred_element_type=jnp.float32)
            * score_scale
        )
        scores = jnp.where(key_live[None, None, :], scores, -1e30)
        new_max = jnp.maximum(running_max, jnp.max(scores, axis=2))
        shrink = jnp.exp(running_max - new_max)
        weights = jnp.exp(scores - new_max[:, :, None]) * key_live[None, None, :].astype(
            jnp.float32
        )
        running_sum = running_sum * shrink + jnp.sum(weights, axis=2)
        running_acc = running_acc * shrink[:, :, None] + jnp.einsum(
            "qhk,khd->qhd",
            weights.astype(jnp.bfloat16),
            value_heads,
            preferred_element_type=jnp.float32,
        )
        return (new_max, running_sum, running_acc)

    stacked = jnp.stack([key_vectors, value_vectors])
    softmax_carry = (
        jnp.full((tokens, head_count), -1e30, jnp.float32),
        jnp.zeros((tokens, head_count), jnp.float32),
        jnp.zeros((tokens, head_count, HEAD_DIM), jnp.float32),
    )
    softmax_carry = absorb(softmax_carry, stacked, query_live)
    if group_size > 1:
        bit_total = group_size.bit_length() - 1

        def make_branch(bit_number):

            def branch(moving):
                return hop_block(moving, bit_number)

            return branch

        branch_list = [make_branch(bit_number) for bit_number in range(bit_total)]

        def cycle_step(step_index, loop_carry):
            inner_carry, moving = loop_carry
            trailing = jnp.int32(0)
            for bit_number in range(bit_total - 1):
                trailing = trailing + (step_index % (2 << bit_number) == 0).astype(jnp.int32)
            moving = lax.switch(trailing, branch_list, moving)
            anchor = jnp.bitwise_xor(group_place, jnp.bitwise_xor(step_index, step_index // 2))
            anchor_count = jnp.sum(jnp.where(members == anchor, counts, 0))
            return (absorb(inner_carry, moving, slot_index < anchor_count), moving)

        softmax_carry, moving = lax.fori_loop(1, group_size, cycle_step, (softmax_carry, stacked))
    running_max, running_sum, running_acc = softmax_carry
    attended = (
        (running_acc / running_sum[:, :, None]).reshape(tokens, feature_width).astype(jnp.bfloat16)
    )
    row_share = tokens // lax.axis_size("tp")
    projected = lax.psum_scatter(
        jnp.dot(attended, proj_weight, preferred_element_type=jnp.float32).astype(jnp.bfloat16),
        "tp",
        scatter_dimension=0,
        tiled=True,
    ).astype(jnp.float32)
    tp_first = lax.axis_index("tp") * row_share
    my_image = lax.dynamic_slice_in_dim(image_mask, tp_first, row_share, 0)
    gate_row = lax.dynamic_index_in_dim(gate_scale, item_index, 0, keepdims=False)
    residual_base = latent.astype(jnp.float32)
    return jnp.where(
        my_image[:, None], residual_base + gate_row[None, :] * projected, residual_base
    ).astype(jnp.bfloat16)


def solution(mesh):
    in_specs = (
        P(("seq", "tp"), None),
        P("seq", "tp"),
        P("seq", "tp"),
        P("seq", "tp"),
        P("tp", None),
        P(),
        P(),
        P(),
    )
    out_specs = P(("seq", "tp"), None)

    def updated(
        latent, queries, key_vectors, value_vectors, proj_weight, gate_scale, text_length, split_table
    ):
        tokens = queries.shape[0] // mesh.shape["seq"]
        whole_request = split_table.shape[1] == 1
        text_first = mesh.shape["tp"] == 4 and tokens // 4 <= LEAST_TEXT
        return jax.shard_map(
            on_device_local if whole_request and text_first else on_device,
            mesh=mesh, in_specs=in_specs, out_specs=out_specs, check_vma=False,
        )(latent, queries, key_vectors, value_vectors, proj_weight, gate_scale, text_length, split_table)

    return updated
```

```python
import functools
import math

import jax
import jax.numpy as jnp
from jax import lax
from jax.experimental import pallas as pl
from jax.experimental.pallas import tpu as pltpu
from jax.sharding import PartitionSpec as P

HEAD_DIM = 128
LEAST_TEXT = 64
CHUNKS = 12
AHEAD = 3
STRIPS = 2
MESH = pl.DeviceIdType.MESH


def local_kernel(
    latent, queries, key_vectors, value_vectors, proj_weight, gate_scale, text_length, split_table,
    base, arrived,
    q_buf, k_buf, v_buf, w_buf, latent_buf, gate_buf, text_buf, table_buf,
    attended, mate_send, mate_recv, kept, far_send, near_send, near_recv, own,
    q_sem, kv_sem, w_sem, small_sem, base_sem,
    mate_sems, far_sems, near_sems,
):
    seq, tp = lax.axis_index("seq"), lax.axis_index("tp")
    core = lax.rem(tp, 2)
    mate = tp + 1 - 2 * core
    far = lax.rem(tp + 2, 4)
    far_mate = lax.rem(mate + 2, 4)
    tokens, width = q_buf.shape
    block = tokens // 4
    heads = width // HEAD_DIM
    columns = w_buf.shape[2]

    barrier = pltpu.get_barrier_semaphore()
    for other in (mate, far):
        pl.semaphore_signal(barrier, inc=1, device_id=(seq, other), device_id_type=MESH)

    q_copies = []
    for place, owner in enumerate((far_mate, far, mate, tp)):
        q_copies.append(
            pltpu.make_async_copy(
                queries.at[pl.ds(pl.multiple_of(owner * block, block), block)],
                q_buf.at[pl.ds(place * block, block)],
                q_sem.at[place],
            )
        )
    k_copy = pltpu.make_async_copy(key_vectors, k_buf, kv_sem.at[0])
    v_copies = [
        pltpu.make_async_copy(
            value_vectors.at[:, pl.ds(head * HEAD_DIM, HEAD_DIM)],
            v_buf.at[:, pl.ds(2 * head * HEAD_DIM, HEAD_DIM)],
            kv_sem.at[1 + head],
        )
        for head in range(heads)
    ]
    table_copy = pltpu.make_async_copy(split_table, table_buf, small_sem.at[0])
    text_copy = pltpu.make_async_copy(text_length, text_buf, small_sem.at[1])
    gate_copy = pltpu.make_async_copy(gate_scale, gate_buf, small_sem.at[2])
    latent_copy = pltpu.make_async_copy(latent, latent_buf, small_sem.at[3])
    w_copies = [
        pltpu.make_async_copy(proj_weight.at[:, pl.ds(i * columns, columns)], w_buf.at[i], w_sem.at[i])
        for i in range(CHUNKS)
    ]
    for copy in (table_copy, k_copy, *q_copies, *v_copies, *w_copies, text_copy, gate_copy, latent_copy):
        copy.start()

    def remote(source, target, sems, i, other):
        return pltpu.make_async_remote_copy(
            src_ref=source.at[i],
            dst_ref=target,
            send_sem=sems.at[0, i],
            recv_sem=sems.at[1, i],
            device_id=(seq, other),
            device_id_type=MESH,
        )

    parts = [pl.ds(i * columns, columns) for i in range(CHUNKS)]
    to_mate = [remote(mate_send, mate_recv.at[i], mate_sems, i, mate) for i in range(CHUNKS)]
    to_far = [remote(far_send, arrived.at[:, parts[i]], far_sems, i, far) for i in range(CHUNKS)]
    to_owner = [remote(near_send, near_recv.at[i], near_sems, i, mate) for i in range(CHUNKS)]
    base_copies = [
        pltpu.make_async_copy(own.at[i], base.at[:, parts[i]], base_sem.at[i]) for i in range(CHUNKS)
    ]

    for head in range(heads):
        v_buf[:, pl.ds((2 * head + 1) * HEAD_DIM, HEAD_DIM)] = jnp.ones((tokens, HEAD_DIM), jnp.bfloat16)

    table_copy.wait()
    count = table_buf[seq]
    key_live = lax.broadcasted_iota(jnp.int32, (1, tokens), 1) < count
    score_scale = math.log2(math.e) / math.sqrt(HEAD_DIM)

    def attend(first, length):
        rows = pl.ds(first, length)
        columns_of = [pl.ds(head * HEAD_DIM, HEAD_DIM) for head in range(heads)]
        scores = [
            lax.dot_general(
                q_buf[rows, part], k_buf[:, part], (((1,), (1,)), ((), ())),
                preferred_element_type=jnp.float32,
            )
            for part in columns_of
        ]
        scores = [jnp.where(key_live, one * score_scale, -1e30) for one in scores]
        weights = [jnp.exp2(one - jnp.max(one, axis=1, keepdims=True)) for one in scores]
        summed = [
            jnp.dot(
                one.astype(jnp.bfloat16), v_buf[:, pl.ds(2 * head * HEAD_DIM, 2 * HEAD_DIM)],
                preferred_element_type=jnp.float32,
            )
            for head, one in enumerate(weights)
        ]
        for part, one in zip(columns_of, summed):
            attended[rows, part] = (one[:, :HEAD_DIM] / one[:, HEAD_DIM:]).astype(jnp.bfloat16)

    k_copy.wait()
    for copy in q_copies:
        copy.wait()
    for copy in v_copies:
        copy.wait()
    def send_to_mate(i, share):
        mate_send[i] = share.astype(jnp.bfloat16)

        @pl.when(tp != 3)
        def _():
            to_mate[i].start()

    def product(first, length, i):
        return jnp.dot(
            attended[pl.ds(first, length), :], w_buf[i], preferred_element_type=jnp.float32
        )

    attend(0, block)
    pl.semaphore_wait(barrier, 2)
    for i in range(AHEAD):
        w_copies[i].wait()
        send_to_mate(i, product(0, block, i))
    attend(block, block)

    text_copy.wait()
    gate_copy.wait()
    latent_copy.wait()
    text = text_buf[seq]

    def image(owner):
        position = owner * block + lax.broadcasted_iota(jnp.int32, (block, 1), 0)
        return (position >= text) & (position < count)

    far_image = image(far)
    for i in range(CHUNKS):
        if i < AHEAD:
            kept[i] = product(block, block, i)

        @pl.when(tp != 2)
        def _():
            to_mate[i].wait_recv()
            summed = kept[i] + mate_recv[i].astype(jnp.float32)
            gated = gate_buf[pl.ds(seq, 1), parts[i]] * summed
            far_send[i] = jnp.where(far_image, gated, 0.0).astype(jnp.bfloat16)
            to_far[i].start()

        later = i + AHEAD
        if later < CHUNKS:
            w_copies[later].wait()
            share = product(0, 2 * block, later)
            kept[later] = share[block:]
            send_to_mate(later, share[:block])

    attend(2 * block, 2 * block)
    for i in range(CHUNKS):
        share = jnp.dot(
            attended[pl.ds(2 * block, 2 * block), :], w_buf[i], preferred_element_type=jnp.float32
        )
        near_send[i] = share[:block].astype(jnp.bfloat16)
        own[i] = share[block:]

        @pl.when(tp != 1)
        def _():
            to_owner[i].start()

    near_image = image(tp)

    @pl.when(tp == 0)
    def _():
        near_recv[...] = jnp.zeros_like(near_recv)
        zero_copies = [
            pltpu.make_async_copy(near_recv.at[i], arrived.at[:, parts[i]], far_sems.at[1, i])
            for i in range(CHUNKS)
        ]
        for i in range(CHUNKS):
            zero_copies[i].start()
            own[i] = latent_buf[:, parts[i]].astype(jnp.float32)
            base_copies[i].start()
        for copy in zero_copies:
            copy.wait()

    @pl.when(tp != 0)
    def _():
        for i in range(CHUNKS):
            to_owner[i].wait_recv()
            projected = own[i] + near_recv[i].astype(jnp.float32)
            residual = latent_buf[:, parts[i]].astype(jnp.float32)
            gate = gate_buf[pl.ds(seq, 1), parts[i]]
            own[i] = jnp.where(near_image, residual + gate * projected, residual)
            base_copies[i].start()
        for i in range(CHUNKS):
            to_far[i].wait_recv()

    for copy in base_copies:
        copy.wait()
    for copies, idle in ((to_mate, 3), (to_far, 2), (to_owner, 1)):

        @pl.when(tp != idle)
        def _():
            for copy in copies:
                copy.wait_send()


def add_kernel(base, arrived, out, base_buf, arrived_buf, out_buf, sems):
    step = out.shape[0] // STRIPS
    rows = [pl.ds(i * step, step) for i in range(STRIPS)]
    loads = [
        (
            pltpu.make_async_copy(arrived.at[part], arrived_buf.at[part], sems.at[0, i]),
            pltpu.make_async_copy(base.at[part], base_buf.at[part], sems.at[1, i]),
        )
        for i, part in enumerate(rows)
    ]
    stores = [
        pltpu.make_async_copy(out_buf.at[part], out.at[part], sems.at[2, i]) for i, part in enumerate(rows)
    ]
    for pair in loads:
        for copy in pair:
            copy.start()
    for part, pair, store in zip(rows, loads, stores):
        for copy in pair:
            copy.wait()
        out_buf[part] = (base_buf[part] + arrived_buf[part].astype(jnp.float32)).astype(jnp.bfloat16)
        store.start()
    for store in stores:
        store.wait()


def on_device_local(
    latent, queries, key_vectors, value_vectors, proj_weight, gate_scale, text_length, split_table
):
    tokens, width = queries.shape
    model = proj_weight.shape[1]
    block, columns = tokens // 4, model // CHUNKS
    in_hbm = pl.BlockSpec(memory_space=pltpu.HBM)
    blocks16 = pltpu.VMEM((CHUNKS, block, columns), jnp.bfloat16)
    blocks32 = pltpu.VMEM((CHUNKS, block, columns), jnp.float32)
    base, arrived = pl.pallas_call(
        local_kernel,
        out_shape=(
            jax.ShapeDtypeStruct(latent.shape, jnp.float32),
            jax.ShapeDtypeStruct(latent.shape, jnp.bfloat16),
        ),
        in_specs=[in_hbm] * 8,
        out_specs=(in_hbm, in_hbm),
        scratch_shapes=[
            pltpu.VMEM((tokens, width), jnp.bfloat16),
            pltpu.VMEM((tokens, width), jnp.bfloat16),
            pltpu.VMEM((tokens, 2 * width), jnp.bfloat16),
            pltpu.VMEM((CHUNKS, width, columns), jnp.bfloat16),
            pltpu.VMEM(latent.shape, jnp.bfloat16),
            pltpu.VMEM(gate_scale.shape, jnp.float32),
            pltpu.SMEM(text_length.shape, jnp.int32),
            pltpu.SMEM((split_table.size,), jnp.int32),
            pltpu.VMEM((tokens, width), jnp.bfloat16),
            blocks16, blocks16, blocks32, blocks16, blocks16, blocks16, blocks32,
            pltpu.SemaphoreType.DMA((4,)),
            pltpu.SemaphoreType.DMA((1 + width // HEAD_DIM,)),
            pltpu.SemaphoreType.DMA((CHUNKS,)),
            pltpu.SemaphoreType.DMA((4,)),
            pltpu.SemaphoreType.DMA((CHUNKS,)),
            pltpu.SemaphoreType.DMA((2, CHUNKS)),
            pltpu.SemaphoreType.DMA((2, CHUNKS)),
            pltpu.SemaphoreType.DMA((2, CHUNKS)),
        ],
        compiler_params=pltpu.CompilerParams(
            collective_id=0, has_side_effects=True, vmem_limit_bytes=64 * 2**20
        ),
        cost_estimate=pl.CostEstimate(
            flops=2 * tokens * width * (model + 2 * tokens), bytes_accessed=4 * 2**20, transcendentals=0
        ),
    )(latent, queries, key_vectors, value_vectors, proj_weight, gate_scale, text_length, split_table.reshape(-1))
    return pl.pallas_call(
        add_kernel,
        out_shape=jax.ShapeDtypeStruct(latent.shape, latent.dtype),
        in_specs=[in_hbm] * 2,
        out_specs=in_hbm,
        scratch_shapes=[
            pltpu.VMEM(latent.shape, jnp.float32),
            pltpu.VMEM(latent.shape, jnp.bfloat16),
            pltpu.VMEM(latent.shape, jnp.bfloat16),
            pltpu.SemaphoreType.DMA((3, STRIPS)),
        ],
        compiler_params=pltpu.CompilerParams(vmem_limit_bytes=64 * 2**20),
        cost_estimate=pl.CostEstimate(flops=latent.size, bytes_accessed=8 * latent.size, transcendentals=0),
    )(base, arrived)


def shortened(shard):
    return jax.tree.map(lambda a: a.astype(jnp.bfloat16) if a.dtype == jnp.float32 else a, shard)


def from_partner(block, axis, stride):
    count = lax.axis_size(axis)
    route = []
    for low in range(count):
        high = low | 1 << stride
        if high != low and high < count:
            route += [(low, high), (high, low)]
    return lax.ppermute(block, axis, route)


def hop_block(moving, bit_number):
    return jax.tree.map(
        lambda part, own: part.astype(own.dtype),
        from_partner(shortened(moving), "seq", bit_number),
        moving,
    )


def on_device(
    latent, queries, key_vectors, value_vectors, proj_weight, gate_scale, text_length, split_table
):
    group_size = split_table.shape[1]
    tokens = queries.shape[0]
    feature_width = queries.shape[1]
    head_count = feature_width // HEAD_DIM
    seq_index = lax.axis_index("seq")
    item_index = seq_index // group_size
    group_place = seq_index % group_size
    counts = lax.dynamic_index_in_dim(split_table, item_index, 0, keepdims=False)
    members = jnp.arange(group_size, dtype=jnp.int32)
    offset = jnp.sum(jnp.where(members < group_place, counts, 0))
    own_count = jnp.sum(jnp.where(members == group_place, counts, 0))
    slot_index = jnp.arange(tokens, dtype=jnp.int32)
    query_live = slot_index < own_count
    text_count = jnp.sum(
        jnp.where(jnp.arange(text_length.shape[0], dtype=jnp.int32) == item_index, text_length, 0)
    )
    image_mask = query_live & (offset + slot_index >= text_count)
    query_heads = queries.reshape(tokens, head_count, HEAD_DIM)
    score_scale = 1.0 / math.sqrt(HEAD_DIM)

    def absorb(softmax_carry, stacked, key_live):
        running_max, running_sum, running_acc = softmax_carry
        length = stacked.shape[1]
        key_heads = stacked[0].reshape(length, head_count, HEAD_DIM)
        value_heads = stacked[1].reshape(length, head_count, HEAD_DIM)
        scores = (
            jnp.einsum("qhd,khd->qhk", query_heads, key_heads, preferred_element_type=jnp.float32)
            * score_scale
        )
        scores = jnp.where(key_live[None, None, :], scores, -1e30)
        new_max = jnp.maximum(running_max, jnp.max(scores, axis=2))
        shrink = jnp.exp(running_max - new_max)
        weights = jnp.exp(scores - new_max[:, :, None]) * key_live[None, None, :].astype(
            jnp.float32
        )
        running_sum = running_sum * shrink + jnp.sum(weights, axis=2)
        running_acc = running_acc * shrink[:, :, None] + jnp.einsum(
            "qhk,khd->qhd",
            weights.astype(jnp.bfloat16),
            value_heads,
            preferred_element_type=jnp.float32,
        )
        return (new_max, running_sum, running_acc)

    stacked = jnp.stack([key_vectors, value_vectors])
    softmax_carry = (
        jnp.full((tokens, head_count), -1e30, jnp.float32),
        jnp.zeros((tokens, head_count), jnp.float32),
        jnp.zeros((tokens, head_count, HEAD_DIM), jnp.float32),
    )
    softmax_carry = absorb(softmax_carry, stacked, query_live)
    if group_size > 1:
        bit_total = group_size.bit_length() - 1

        def make_branch(bit_number):

            def branch(moving):
                return hop_block(moving, bit_number)

            return branch

        branch_list = [make_branch(bit_number) for bit_number in range(bit_total)]

        def cycle_step(step_index, loop_carry):
            inner_carry, moving = loop_carry
            trailing = jnp.int32(0)
            for bit_number in range(bit_total - 1):
                trailing = trailing + (step_index % (2 << bit_number) == 0).astype(jnp.int32)
            moving = lax.switch(trailing, branch_list, moving)
            anchor = jnp.bitwise_xor(group_place, jnp.bitwise_xor(step_index, step_index // 2))
            anchor_count = jnp.sum(jnp.where(members == anchor, counts, 0))
            return (absorb(inner_carry, moving, slot_index < anchor_count), moving)

        softmax_carry, moving = lax.fori_loop(1, group_size, cycle_step, (softmax_carry, stacked))
    running_max, running_sum, running_acc = softmax_carry
    attended = (
        (running_acc / running_sum[:, :, None]).reshape(tokens, feature_width).astype(jnp.bfloat16)
    )
    row_share = tokens // lax.axis_size("tp")
    projected = lax.psum_scatter(
        jnp.dot(attended, proj_weight, preferred_element_type=jnp.float32).astype(jnp.bfloat16),
        "tp",
        scatter_dimension=0,
        tiled=True,
    ).astype(jnp.float32)
    tp_first = lax.axis_index("tp") * row_share
    my_image = lax.dynamic_slice_in_dim(image_mask, tp_first, row_share, 0)
    gate_row = lax.dynamic_index_in_dim(gate_scale, item_index, 0, keepdims=False)
    residual_base = latent.astype(jnp.float32)
    return jnp.where(
        my_image[:, None], residual_base + gate_row[None, :] * projected, residual_base
    ).astype(jnp.bfloat16)


def solution(mesh):
    in_specs = (
        P(("seq", "tp"), None),
        P("seq", "tp"),
        P("seq", "tp"),
        P("seq", "tp"),
        P("tp", None),
        P(),
        P(),
        P(),
    )
    out_specs = P(("seq", "tp"), None)

    def updated(
        latent, queries, key_vectors, value_vectors, proj_weight, gate_scale, text_length, split_table
    ):
        tokens = queries.shape[0] // mesh.shape["seq"]
        whole_request = split_table.shape[1] == 1
        text_first = mesh.shape["tp"] == 4 and tokens // 4 <= LEAST_TEXT
        return jax.shard_map(
            on_device_local if whole_request and text_first else on_device,
            mesh=mesh, in_specs=in_specs, out_specs=out_specs, check_vma=False,
        )(latent, queries, key_vectors, value_vectors, proj_weight, gate_scale, text_length, split_table)

    return updated
```

```python
import functools
import math

import jax
import jax.numpy as jnp
from jax import lax
from jax.experimental import pallas as pl
from jax.experimental.pallas import tpu as pltpu
from jax.sharding import PartitionSpec as P

HEAD_DIM = 128
LEAST_TEXT = 64
CHUNKS = 12
AHEAD = 3
MESH = pl.DeviceIdType.MESH


def local_kernel(
    latent, queries, key_vectors, value_vectors, proj_weight, gate_scale, text_length, split_table,
    base, arrived,
    q_buf, k_buf, v_buf, w_buf, latent_buf, gate_buf, text_buf, table_buf,
    attended, mate_send, mate_recv, kept, far_send, near_send, near_recv, own,
    q_sem, kv_sem, w_sem, small_sem, base_sem,
    mate_sems, far_sems, near_sems,
):
    seq, tp = lax.axis_index("seq"), lax.axis_index("tp")
    core = lax.rem(tp, 2)
    mate = tp + 1 - 2 * core
    far = lax.rem(tp + 2, 4)
    far_mate = lax.rem(mate + 2, 4)
    tokens, width = q_buf.shape
    block = tokens // 4
    heads = width // HEAD_DIM
    columns = w_buf.shape[2]

    barrier = pltpu.get_barrier_semaphore()
    for other in (mate, far):
        pl.semaphore_signal(barrier, inc=1, device_id=(seq, other), device_id_type=MESH)

    q_copies = []
    for place, owner in enumerate((far_mate, far, mate, tp)):
        q_copies.append(
            pltpu.make_async_copy(
                queries.at[pl.ds(pl.multiple_of(owner * block, block), block)],
                q_buf.at[pl.ds(place * block, block)],
                q_sem.at[place],
            )
        )
    k_copy = pltpu.make_async_copy(key_vectors, k_buf, kv_sem.at[0])
    v_copies = [
        pltpu.make_async_copy(
            value_vectors.at[:, pl.ds(head * HEAD_DIM, HEAD_DIM)],
            v_buf.at[:, pl.ds(2 * head * HEAD_DIM, HEAD_DIM)],
            kv_sem.at[1 + head],
        )
        for head in range(heads)
    ]
    table_copy = pltpu.make_async_copy(split_table, table_buf, small_sem.at[0])
    text_copy = pltpu.make_async_copy(text_length, text_buf, small_sem.at[1])
    gate_copy = pltpu.make_async_copy(gate_scale, gate_buf, small_sem.at[2])
    latent_copy = pltpu.make_async_copy(latent, latent_buf, small_sem.at[3])
    w_copies = [
        pltpu.make_async_copy(proj_weight.at[:, pl.ds(i * columns, columns)], w_buf.at[i], w_sem.at[i])
        for i in range(CHUNKS)
    ]
    for copy in (table_copy, *q_copies, k_copy, *v_copies, text_copy, gate_copy, *w_copies, latent_copy):
        copy.start()

    def remote(source, target, sems, i, other):
        return pltpu.make_async_remote_copy(
            src_ref=source.at[i],
            dst_ref=target,
            send_sem=sems.at[0, i],
            recv_sem=sems.at[1, i],
            device_id=(seq, other),
            device_id_type=MESH,
        )

    parts = [pl.ds(i * columns, columns) for i in range(CHUNKS)]
    to_mate = [remote(mate_send, mate_recv.at[i], mate_sems, i, mate) for i in range(CHUNKS)]
    to_far = [remote(far_send, arrived.at[:, parts[i]], far_sems, i, far) for i in range(CHUNKS)]
    to_owner = [remote(near_send, near_recv.at[i], near_sems, i, mate) for i in range(CHUNKS)]
    base_copies = [
        pltpu.make_async_copy(own.at[i], base.at[:, parts[i]], base_sem.at[i]) for i in range(CHUNKS)
    ]

    for head in range(heads):
        v_buf[:, pl.ds((2 * head + 1) * HEAD_DIM, HEAD_DIM)] = jnp.ones((tokens, HEAD_DIM), jnp.bfloat16)

    table_copy.wait()
    count = table_buf[seq]
    key_live = lax.broadcasted_iota(jnp.int32, (1, tokens), 1) < count
    score_scale = math.log2(math.e) / math.sqrt(HEAD_DIM)

    def attend(first, length):
        rows = pl.ds(first, length)
        columns_of = [pl.ds(head * HEAD_DIM, HEAD_DIM) for head in range(heads)]
        scores = [
            lax.dot_general(
                q_buf[rows, part], k_buf[:, part], (((1,), (1,)), ((), ())),
                preferred_element_type=jnp.float32,
            )
            for part in columns_of
        ]
        scores = [jnp.where(key_live, one * score_scale, -1e30) for one in scores]
        weights = [jnp.exp2(one - jnp.max(one, axis=1, keepdims=True)) for one in scores]
        summed = [
            jnp.dot(
                one.astype(jnp.bfloat16), v_buf[:, pl.ds(2 * head * HEAD_DIM, 2 * HEAD_DIM)],
                preferred_element_type=jnp.float32,
            )
            for head, one in enumerate(weights)
        ]
        for part, one in zip(columns_of, summed):
            attended[rows, part] = (one[:, :HEAD_DIM] / one[:, HEAD_DIM:]).astype(jnp.bfloat16)

    k_copy.wait()
    for copy in q_copies:
        copy.wait()
    for copy in v_copies:
        copy.wait()
    def send_to_mate(i, share):
        mate_send[i] = share.astype(jnp.bfloat16)

        @pl.when(tp != 3)
        def _():
            to_mate[i].start()

    def product(first, length, i):
        return jnp.dot(
            attended[pl.ds(first, length), :], w_buf[i], preferred_element_type=jnp.float32
        )

    attend(0, block)
    pl.semaphore_wait(barrier, 2)
    for i in range(AHEAD):
        w_copies[i].wait()
        send_to_mate(i, product(0, block, i))
    attend(block, block)

    text_copy.wait()
    gate_copy.wait()
    text = text_buf[seq]

    def image(owner):
        position = owner * block + lax.broadcasted_iota(jnp.int32, (block, 1), 0)
        return (position >= text) & (position < count)

    far_image = image(far)
    for i in range(CHUNKS):
        if i < AHEAD:
            kept[i] = product(block, block, i)

        @pl.when(tp != 2)
        def _():
            to_mate[i].wait_recv()
            summed = kept[i] + mate_recv[i].astype(jnp.float32)
            gated = gate_buf[pl.ds(seq, 1), parts[i]] * summed
            far_send[i] = jnp.where(far_image, gated, 0.0).astype(jnp.bfloat16)
            to_far[i].start()

        later = i + AHEAD
        if later < CHUNKS:
            w_copies[later].wait()
            share = product(0, 2 * block, later)
            kept[later] = share[block:]
            send_to_mate(later, share[:block])

    attend(2 * block, 2 * block)
    for i in range(CHUNKS):
        share = jnp.dot(
            attended[pl.ds(2 * block, 2 * block), :], w_buf[i], preferred_element_type=jnp.float32
        )
        near_send[i] = share[:block].astype(jnp.bfloat16)
        own[i] = share[block:]

        @pl.when(tp != 1)
        def _():
            to_owner[i].start()

    latent_copy.wait()
    near_image = image(tp)

    @pl.when(tp == 0)
    def _():
        near_recv[...] = jnp.zeros_like(near_recv)
        zero_copies = [
            pltpu.make_async_copy(near_recv.at[i], arrived.at[:, parts[i]], far_sems.at[1, i])
            for i in range(CHUNKS)
        ]
        for i in range(CHUNKS):
            zero_copies[i].start()
            own[i] = latent_buf[:, parts[i]].astype(jnp.float32)
            base_copies[i].start()
        for copy in zero_copies:
            copy.wait()

    @pl.when(tp != 0)
    def _():
        for i in range(CHUNKS):
            to_owner[i].wait_recv()
            projected = own[i] + near_recv[i].astype(jnp.float32)
            residual = latent_buf[:, parts[i]].astype(jnp.float32)
            gate = gate_buf[pl.ds(seq, 1), parts[i]]
            own[i] = jnp.where(near_image, residual + gate * projected, residual)
            base_copies[i].start()
        for i in range(CHUNKS):
            to_far[i].wait_recv()

    for copy in base_copies:
        copy.wait()
    for copies, idle in ((to_mate, 3), (to_far, 2), (to_owner, 1)):

        @pl.when(tp != idle)
        def _():
            for copy in copies:
                copy.wait_send()


def on_device_local(
    latent, queries, key_vectors, value_vectors, proj_weight, gate_scale, text_length, split_table
):
    tokens, width = queries.shape
    model = proj_weight.shape[1]
    block, columns = tokens // 4, model // CHUNKS
    in_hbm = pl.BlockSpec(memory_space=pltpu.HBM)
    blocks16 = pltpu.VMEM((CHUNKS, block, columns), jnp.bfloat16)
    blocks32 = pltpu.VMEM((CHUNKS, block, columns), jnp.float32)
    base, arrived = pl.pallas_call(
        local_kernel,
        out_shape=(
            jax.ShapeDtypeStruct(latent.shape, jnp.float32),
            jax.ShapeDtypeStruct(latent.shape, jnp.bfloat16),
        ),
        in_specs=[in_hbm] * 8,
        out_specs=(in_hbm, in_hbm),
        scratch_shapes=[
            pltpu.VMEM((tokens, width), jnp.bfloat16),
            pltpu.VMEM((tokens, width), jnp.bfloat16),
            pltpu.VMEM((tokens, 2 * width), jnp.bfloat16),
            pltpu.VMEM((CHUNKS, width, columns), jnp.bfloat16),
            pltpu.VMEM(latent.shape, jnp.bfloat16),
            pltpu.VMEM(gate_scale.shape, jnp.float32),
            pltpu.SMEM(text_length.shape, jnp.int32),
            pltpu.SMEM((split_table.size,), jnp.int32),
            pltpu.VMEM((tokens, width), jnp.bfloat16),
            blocks16, blocks16, blocks32, blocks16, blocks16, blocks16, blocks32,
            pltpu.SemaphoreType.DMA((4,)),
            pltpu.SemaphoreType.DMA((1 + width // HEAD_DIM,)),
            pltpu.SemaphoreType.DMA((CHUNKS,)),
            pltpu.SemaphoreType.DMA((4,)),
            pltpu.SemaphoreType.DMA((CHUNKS,)),
            pltpu.SemaphoreType.DMA((2, CHUNKS)),
            pltpu.SemaphoreType.DMA((2, CHUNKS)),
            pltpu.SemaphoreType.DMA((2, CHUNKS)),
        ],
        compiler_params=pltpu.CompilerParams(
            collective_id=0, has_side_effects=True, vmem_limit_bytes=64 * 2**20
        ),
        cost_estimate=pl.CostEstimate(
            flops=2 * tokens * width * (model + 2 * tokens), bytes_accessed=4 * 2**20, transcendentals=0
        ),
    )(latent, queries, key_vectors, value_vectors, proj_weight, gate_scale, text_length, split_table.reshape(-1))
    return (base + arrived.astype(jnp.float32)).astype(jnp.bfloat16)


def shortened(shard):
    return jax.tree.map(lambda a: a.astype(jnp.bfloat16) if a.dtype == jnp.float32 else a, shard)


def from_partner(block, axis, stride):
    count = lax.axis_size(axis)
    route = []
    for low in range(count):
        high = low | 1 << stride
        if high != low and high < count:
            route += [(low, high), (high, low)]
    return lax.ppermute(block, axis, route)


def hop_block(moving, bit_number):
    return jax.tree.map(
        lambda part, own: part.astype(own.dtype),
        from_partner(shortened(moving), "seq", bit_number),
        moving,
    )


def on_device(
    latent, queries, key_vectors, value_vectors, proj_weight, gate_scale, text_length, split_table
):
    group_size = split_table.shape[1]
    tokens = queries.shape[0]
    feature_width = queries.shape[1]
    head_count = feature_width // HEAD_DIM
    seq_index = lax.axis_index("seq")
    item_index = seq_index // group_size
    group_place = seq_index % group_size
    counts = lax.dynamic_index_in_dim(split_table, item_index, 0, keepdims=False)
    members = jnp.arange(group_size, dtype=jnp.int32)
    offset = jnp.sum(jnp.where(members < group_place, counts, 0))
    own_count = jnp.sum(jnp.where(members == group_place, counts, 0))
    slot_index = jnp.arange(tokens, dtype=jnp.int32)
    query_live = slot_index < own_count
    text_count = jnp.sum(
        jnp.where(jnp.arange(text_length.shape[0], dtype=jnp.int32) == item_index, text_length, 0)
    )
    image_mask = query_live & (offset + slot_index >= text_count)
    query_heads = queries.reshape(tokens, head_count, HEAD_DIM)
    score_scale = 1.0 / math.sqrt(HEAD_DIM)

    def absorb(softmax_carry, stacked, key_live):
        running_max, running_sum, running_acc = softmax_carry
        length = stacked.shape[1]
        key_heads = stacked[0].reshape(length, head_count, HEAD_DIM)
        value_heads = stacked[1].reshape(length, head_count, HEAD_DIM)
        scores = (
            jnp.einsum("qhd,khd->qhk", query_heads, key_heads, preferred_element_type=jnp.float32)
            * score_scale
        )
        scores = jnp.where(key_live[None, None, :], scores, -1e30)
        new_max = jnp.maximum(running_max, jnp.max(scores, axis=2))
        shrink = jnp.exp(running_max - new_max)
        weights = jnp.exp(scores - new_max[:, :, None]) * key_live[None, None, :].astype(
            jnp.float32
        )
        running_sum = running_sum * shrink + jnp.sum(weights, axis=2)
        running_acc = running_acc * shrink[:, :, None] + jnp.einsum(
            "qhk,khd->qhd",
            weights.astype(jnp.bfloat16),
            value_heads,
            preferred_element_type=jnp.float32,
        )
        return (new_max, running_sum, running_acc)

    stacked = jnp.stack([key_vectors, value_vectors])
    softmax_carry = (
        jnp.full((tokens, head_count), -1e30, jnp.float32),
        jnp.zeros((tokens, head_count), jnp.float32),
        jnp.zeros((tokens, head_count, HEAD_DIM), jnp.float32),
    )
    softmax_carry = absorb(softmax_carry, stacked, query_live)
    if group_size > 1:
        bit_total = group_size.bit_length() - 1

        def make_branch(bit_number):

            def branch(moving):
                return hop_block(moving, bit_number)

            return branch

        branch_list = [make_branch(bit_number) for bit_number in range(bit_total)]

        def cycle_step(step_index, loop_carry):
            inner_carry, moving = loop_carry
            trailing = jnp.int32(0)
            for bit_number in range(bit_total - 1):
                trailing = trailing + (step_index % (2 << bit_number) == 0).astype(jnp.int32)
            moving = lax.switch(trailing, branch_list, moving)
            anchor = jnp.bitwise_xor(group_place, jnp.bitwise_xor(step_index, step_index // 2))
            anchor_count = jnp.sum(jnp.where(members == anchor, counts, 0))
            return (absorb(inner_carry, moving, slot_index < anchor_count), moving)

        softmax_carry, moving = lax.fori_loop(1, group_size, cycle_step, (softmax_carry, stacked))
    running_max, running_sum, running_acc = softmax_carry
    attended = (
        (running_acc / running_sum[:, :, None]).reshape(tokens, feature_width).astype(jnp.bfloat16)
    )
    row_share = tokens // lax.axis_size("tp")
    projected = lax.psum_scatter(
        jnp.dot(attended, proj_weight, preferred_element_type=jnp.float32).astype(jnp.bfloat16),
        "tp",
        scatter_dimension=0,
        tiled=True,
    ).astype(jnp.float32)
    tp_first = lax.axis_index("tp") * row_share
    my_image = lax.dynamic_slice_in_dim(image_mask, tp_first, row_share, 0)
    gate_row = lax.dynamic_index_in_dim(gate_scale, item_index, 0, keepdims=False)
    residual_base = latent.astype(jnp.float32)
    return jnp.where(
        my_image[:, None], residual_base + gate_row[None, :] * projected, residual_base
    ).astype(jnp.bfloat16)


def solution(mesh):
    in_specs = (
        P(("seq", "tp"), None),
        P("seq", "tp"),
        P("seq", "tp"),
        P("seq", "tp"),
        P("tp", None),
        P(),
        P(),
        P(),
    )
    out_specs = P(("seq", "tp"), None)

    def updated(
        latent, queries, key_vectors, value_vectors, proj_weight, gate_scale, text_length, split_table
    ):
        tokens = queries.shape[0] // mesh.shape["seq"]
        whole_request = split_table.shape[1] == 1
        text_first = mesh.shape["tp"] == 4 and tokens // 4 <= LEAST_TEXT
        return jax.shard_map(
            on_device_local if whole_request and text_first else on_device,
            mesh=mesh, in_specs=in_specs, out_specs=out_specs, check_vma=False,
        )(latent, queries, key_vectors, value_vectors, proj_weight, gate_scale, text_length, split_table)

    return updated
```

```python
import functools
import math

import jax
import jax.numpy as jnp
from jax import lax
from jax.experimental import pallas as pl
from jax.experimental.pallas import tpu as pltpu
from jax.sharding import PartitionSpec as P

HEAD_DIM = 128
LEAST_TEXT = 64
CHUNKS = 6
AHEAD = 2
MESH = pl.DeviceIdType.MESH


def local_kernel(
    latent, queries, key_vectors, value_vectors, proj_weight, gate_scale, text_length, split_table,
    base, arrived,
    q_buf, k_buf, v_buf, w_buf, latent_buf, gate_buf, text_buf, table_buf,
    attended, mate_send, mate_recv, kept, far_send, near_send, near_recv, own,
    q_sem, kv_sem, w_sem, small_sem, base_sem,
    mate_sems, far_sems, near_sems,
):
    seq, tp = lax.axis_index("seq"), lax.axis_index("tp")
    core = lax.rem(tp, 2)
    mate = tp + 1 - 2 * core
    far = lax.rem(tp + 2, 4)
    far_mate = lax.rem(mate + 2, 4)
    tokens, width = q_buf.shape
    block = tokens // 4
    heads = width // HEAD_DIM
    columns = w_buf.shape[2]

    barrier = pltpu.get_barrier_semaphore()
    for other in (mate, far):
        pl.semaphore_signal(barrier, inc=1, device_id=(seq, other), device_id_type=MESH)

    q_copies = []
    for place, owner in enumerate((far_mate, far, mate, tp)):
        q_copies.append(
            pltpu.make_async_copy(
                queries.at[pl.ds(pl.multiple_of(owner * block, block), block)],
                q_buf.at[pl.ds(place * block, block)],
                q_sem.at[place],
            )
        )
    k_copy = pltpu.make_async_copy(key_vectors, k_buf, kv_sem.at[0])
    v_copies = [
        pltpu.make_async_copy(
            value_vectors.at[:, pl.ds(head * HEAD_DIM, HEAD_DIM)],
            v_buf.at[:, pl.ds(2 * head * HEAD_DIM, HEAD_DIM)],
            kv_sem.at[1 + head],
        )
        for head in range(heads)
    ]
    table_copy = pltpu.make_async_copy(split_table, table_buf, small_sem.at[0])
    text_copy = pltpu.make_async_copy(text_length, text_buf, small_sem.at[1])
    gate_copy = pltpu.make_async_copy(gate_scale, gate_buf, small_sem.at[2])
    latent_copy = pltpu.make_async_copy(latent, latent_buf, small_sem.at[3])
    w_copies = [
        pltpu.make_async_copy(proj_weight.at[:, pl.ds(i * columns, columns)], w_buf.at[i], w_sem.at[i])
        for i in range(CHUNKS)
    ]
    for copy in (table_copy, *q_copies, k_copy, *v_copies, text_copy, gate_copy, *w_copies, latent_copy):
        copy.start()

    def remote(source, target, sems, i, other):
        return pltpu.make_async_remote_copy(
            src_ref=source.at[i],
            dst_ref=target,
            send_sem=sems.at[0, i],
            recv_sem=sems.at[1, i],
            device_id=(seq, other),
            device_id_type=MESH,
        )

    parts = [pl.ds(i * columns, columns) for i in range(CHUNKS)]
    to_mate = [remote(mate_send, mate_recv.at[i], mate_sems, i, mate) for i in range(CHUNKS)]
    to_far = [remote(far_send, arrived.at[:, parts[i]], far_sems, i, far) for i in range(CHUNKS)]
    to_owner = [remote(near_send, near_recv.at[i], near_sems, i, mate) for i in range(CHUNKS)]
    base_copies = [
        pltpu.make_async_copy(own.at[i], base.at[:, parts[i]], base_sem.at[i]) for i in range(CHUNKS)
    ]

    for head in range(heads):
        v_buf[:, pl.ds((2 * head + 1) * HEAD_DIM, HEAD_DIM)] = jnp.ones((tokens, HEAD_DIM), jnp.bfloat16)

    table_copy.wait()
    count = table_buf[seq]
    key_live = lax.broadcasted_iota(jnp.int32, (1, tokens), 1) < count
    score_scale = math.log2(math.e) / math.sqrt(HEAD_DIM)

    def attend(first, length):
        rows = pl.ds(first, length)
        columns_of = [pl.ds(head * HEAD_DIM, HEAD_DIM) for head in range(heads)]
        scores = [
            lax.dot_general(
                q_buf[rows, part], k_buf[:, part], (((1,), (1,)), ((), ())),
                preferred_element_type=jnp.float32,
            )
            for part in columns_of
        ]
        scores = [jnp.where(key_live, one * score_scale, -1e30) for one in scores]
        weights = [jnp.exp2(one - jnp.max(one, axis=1, keepdims=True)) for one in scores]
        summed = [
            jnp.dot(
                one.astype(jnp.bfloat16), v_buf[:, pl.ds(2 * head * HEAD_DIM, 2 * HEAD_DIM)],
                preferred_element_type=jnp.float32,
            )
            for head, one in enumerate(weights)
        ]
        for part, one in zip(columns_of, summed):
            attended[rows, part] = (one[:, :HEAD_DIM] / one[:, HEAD_DIM:]).astype(jnp.bfloat16)

    k_copy.wait()
    for copy in q_copies:
        copy.wait()
    for copy in v_copies:
        copy.wait()
    def send_to_mate(i, share):
        mate_send[i] = share.astype(jnp.bfloat16)

        @pl.when(tp != 3)
        def _():
            to_mate[i].start()

    def product(first, length, i):
        return jnp.dot(
            attended[pl.ds(first, length), :], w_buf[i], preferred_element_type=jnp.float32
        )

    attend(0, block)
    pl.semaphore_wait(barrier, 2)
    for i in range(AHEAD):
        w_copies[i].wait()
        send_to_mate(i, product(0, block, i))
    attend(block, block)

    text_copy.wait()
    gate_copy.wait()
    text = text_buf[seq]

    def image(owner):
        position = owner * block + lax.broadcasted_iota(jnp.int32, (block, 1), 0)
        return (position >= text) & (position < count)

    far_image = image(far)
    for i in range(CHUNKS):
        if i < AHEAD:
            kept[i] = product(block, block, i)

        @pl.when(tp != 2)
        def _():
            to_mate[i].wait_recv()
            summed = kept[i] + mate_recv[i].astype(jnp.float32)
            gated = gate_buf[pl.ds(seq, 1), parts[i]] * summed
            far_send[i] = jnp.where(far_image, gated, 0.0).astype(jnp.bfloat16)
            to_far[i].start()

        later = i + AHEAD
        if later < CHUNKS:
            w_copies[later].wait()
            share = product(0, 2 * block, later)
            kept[later] = share[block:]
            send_to_mate(later, share[:block])

    attend(2 * block, 2 * block)
    for i in range(CHUNKS):
        share = jnp.dot(
            attended[pl.ds(2 * block, 2 * block), :], w_buf[i], preferred_element_type=jnp.float32
        )
        near_send[i] = share[:block].astype(jnp.bfloat16)
        own[i] = share[block:]

        @pl.when(tp != 1)
        def _():
            to_owner[i].start()

    latent_copy.wait()
    near_image = image(tp)

    @pl.when(tp == 0)
    def _():
        near_recv[...] = jnp.zeros_like(near_recv)
        zero_copies = [
            pltpu.make_async_copy(near_recv.at[i], arrived.at[:, parts[i]], far_sems.at[1, i])
            for i in range(CHUNKS)
        ]
        for i in range(CHUNKS):
            zero_copies[i].start()
            own[i] = latent_buf[:, parts[i]].astype(jnp.float32)
            base_copies[i].start()
        for copy in zero_copies:
            copy.wait()

    @pl.when(tp != 0)
    def _():
        for i in range(CHUNKS):
            to_owner[i].wait_recv()
            projected = own[i] + near_recv[i].astype(jnp.float32)
            residual = latent_buf[:, parts[i]].astype(jnp.float32)
            gate = gate_buf[pl.ds(seq, 1), parts[i]]
            own[i] = jnp.where(near_image, residual + gate * projected, residual)
            base_copies[i].start()
        for i in range(CHUNKS):
            to_far[i].wait_recv()

    for copy in base_copies:
        copy.wait()
    for copies, idle in ((to_mate, 3), (to_far, 2), (to_owner, 1)):

        @pl.when(tp != idle)
        def _():
            for copy in copies:
                copy.wait_send()


def on_device_local(
    latent, queries, key_vectors, value_vectors, proj_weight, gate_scale, text_length, split_table
):
    tokens, width = queries.shape
    model = proj_weight.shape[1]
    block, columns = tokens // 4, model // CHUNKS
    in_hbm = pl.BlockSpec(memory_space=pltpu.HBM)
    blocks16 = pltpu.VMEM((CHUNKS, block, columns), jnp.bfloat16)
    blocks32 = pltpu.VMEM((CHUNKS, block, columns), jnp.float32)
    base, arrived = pl.pallas_call(
        local_kernel,
        out_shape=(
            jax.ShapeDtypeStruct(latent.shape, jnp.float32),
            jax.ShapeDtypeStruct(latent.shape, jnp.bfloat16),
        ),
        in_specs=[in_hbm] * 8,
        out_specs=(in_hbm, in_hbm),
        scratch_shapes=[
            pltpu.VMEM((tokens, width), jnp.bfloat16),
            pltpu.VMEM((tokens, width), jnp.bfloat16),
            pltpu.VMEM((tokens, 2 * width), jnp.bfloat16),
            pltpu.VMEM((CHUNKS, width, columns), jnp.bfloat16),
            pltpu.VMEM(latent.shape, jnp.bfloat16),
            pltpu.VMEM(gate_scale.shape, jnp.float32),
            pltpu.SMEM(text_length.shape, jnp.int32),
            pltpu.SMEM((split_table.size,), jnp.int32),
            pltpu.VMEM((tokens, width), jnp.bfloat16),
            blocks16, blocks16, blocks32, blocks16, blocks16, blocks16, blocks32,
            pltpu.SemaphoreType.DMA((4,)),
            pltpu.SemaphoreType.DMA((1 + width // HEAD_DIM,)),
            pltpu.SemaphoreType.DMA((CHUNKS,)),
            pltpu.SemaphoreType.DMA((4,)),
            pltpu.SemaphoreType.DMA((CHUNKS,)),
            pltpu.SemaphoreType.DMA((2, CHUNKS)),
            pltpu.SemaphoreType.DMA((2, CHUNKS)),
            pltpu.SemaphoreType.DMA((2, CHUNKS)),
        ],
        compiler_params=pltpu.CompilerParams(
            collective_id=0, has_side_effects=True, vmem_limit_bytes=64 * 2**20
        ),
        cost_estimate=pl.CostEstimate(
            flops=2 * tokens * width * (model + 2 * tokens), bytes_accessed=4 * 2**20, transcendentals=0
        ),
    )(latent, queries, key_vectors, value_vectors, proj_weight, gate_scale, text_length, split_table.reshape(-1))
    return (base + arrived.astype(jnp.float32)).astype(jnp.bfloat16)


def shortened(shard):
    return jax.tree.map(lambda a: a.astype(jnp.bfloat16) if a.dtype == jnp.float32 else a, shard)


def from_partner(block, axis, stride):
    count = lax.axis_size(axis)
    route = []
    for low in range(count):
        high = low | 1 << stride
        if high != low and high < count:
            route += [(low, high), (high, low)]
    return lax.ppermute(block, axis, route)


def hop_block(moving, bit_number):
    return jax.tree.map(
        lambda part, own: part.astype(own.dtype),
        from_partner(shortened(moving), "seq", bit_number),
        moving,
    )


def on_device(
    latent, queries, key_vectors, value_vectors, proj_weight, gate_scale, text_length, split_table
):
    group_size = split_table.shape[1]
    tokens = queries.shape[0]
    feature_width = queries.shape[1]
    head_count = feature_width // HEAD_DIM
    seq_index = lax.axis_index("seq")
    item_index = seq_index // group_size
    group_place = seq_index % group_size
    counts = lax.dynamic_index_in_dim(split_table, item_index, 0, keepdims=False)
    members = jnp.arange(group_size, dtype=jnp.int32)
    offset = jnp.sum(jnp.where(members < group_place, counts, 0))
    own_count = jnp.sum(jnp.where(members == group_place, counts, 0))
    slot_index = jnp.arange(tokens, dtype=jnp.int32)
    query_live = slot_index < own_count
    text_count = jnp.sum(
        jnp.where(jnp.arange(text_length.shape[0], dtype=jnp.int32) == item_index, text_length, 0)
    )
    image_mask = query_live & (offset + slot_index >= text_count)
    query_heads = queries.reshape(tokens, head_count, HEAD_DIM)
    score_scale = 1.0 / math.sqrt(HEAD_DIM)

    def absorb(softmax_carry, stacked, key_live):
        running_max, running_sum, running_acc = softmax_carry
        length = stacked.shape[1]
        key_heads = stacked[0].reshape(length, head_count, HEAD_DIM)
        value_heads = stacked[1].reshape(length, head_count, HEAD_DIM)
        scores = (
            jnp.einsum("qhd,khd->qhk", query_heads, key_heads, preferred_element_type=jnp.float32)
            * score_scale
        )
        scores = jnp.where(key_live[None, None, :], scores, -1e30)
        new_max = jnp.maximum(running_max, jnp.max(scores, axis=2))
        shrink = jnp.exp(running_max - new_max)
        weights = jnp.exp(scores - new_max[:, :, None]) * key_live[None, None, :].astype(
            jnp.float32
        )
        running_sum = running_sum * shrink + jnp.sum(weights, axis=2)
        running_acc = running_acc * shrink[:, :, None] + jnp.einsum(
            "qhk,khd->qhd",
            weights.astype(jnp.bfloat16),
            value_heads,
            preferred_element_type=jnp.float32,
        )
        return (new_max, running_sum, running_acc)

    stacked = jnp.stack([key_vectors, value_vectors])
    softmax_carry = (
        jnp.full((tokens, head_count), -1e30, jnp.float32),
        jnp.zeros((tokens, head_count), jnp.float32),
        jnp.zeros((tokens, head_count, HEAD_DIM), jnp.float32),
    )
    softmax_carry = absorb(softmax_carry, stacked, query_live)
    if group_size > 1:
        bit_total = group_size.bit_length() - 1

        def make_branch(bit_number):

            def branch(moving):
                return hop_block(moving, bit_number)

            return branch

        branch_list = [make_branch(bit_number) for bit_number in range(bit_total)]

        def cycle_step(step_index, loop_carry):
            inner_carry, moving = loop_carry
            trailing = jnp.int32(0)
            for bit_number in range(bit_total - 1):
                trailing = trailing + (step_index % (2 << bit_number) == 0).astype(jnp.int32)
            moving = lax.switch(trailing, branch_list, moving)
            anchor = jnp.bitwise_xor(group_place, jnp.bitwise_xor(step_index, step_index // 2))
            anchor_count = jnp.sum(jnp.where(members == anchor, counts, 0))
            return (absorb(inner_carry, moving, slot_index < anchor_count), moving)

        softmax_carry, moving = lax.fori_loop(1, group_size, cycle_step, (softmax_carry, stacked))
    running_max, running_sum, running_acc = softmax_carry
    attended = (
        (running_acc / running_sum[:, :, None]).reshape(tokens, feature_width).astype(jnp.bfloat16)
    )
    row_share = tokens // lax.axis_size("tp")
    projected = lax.psum_scatter(
        jnp.dot(attended, proj_weight, preferred_element_type=jnp.float32).astype(jnp.bfloat16),
        "tp",
        scatter_dimension=0,
        tiled=True,
    ).astype(jnp.float32)
    tp_first = lax.axis_index("tp") * row_share
    my_image = lax.dynamic_slice_in_dim(image_mask, tp_first, row_share, 0)
    gate_row = lax.dynamic_index_in_dim(gate_scale, item_index, 0, keepdims=False)
    residual_base = latent.astype(jnp.float32)
    return jnp.where(
        my_image[:, None], residual_base + gate_row[None, :] * projected, residual_base
    ).astype(jnp.bfloat16)


def solution(mesh):
    in_specs = (
        P(("seq", "tp"), None),
        P("seq", "tp"),
        P("seq", "tp"),
        P("seq", "tp"),
        P("tp", None),
        P(),
        P(),
        P(),
    )
    out_specs = P(("seq", "tp"), None)

    def updated(
        latent, queries, key_vectors, value_vectors, proj_weight, gate_scale, text_length, split_table
    ):
        tokens = queries.shape[0] // mesh.shape["seq"]
        whole_request = split_table.shape[1] == 1
        text_first = mesh.shape["tp"] == 4 and tokens // 4 <= LEAST_TEXT
        return jax.shard_map(
            on_device_local if whole_request and text_first else on_device,
            mesh=mesh, in_specs=in_specs, out_specs=out_specs, check_vma=False,
        )(latent, queries, key_vectors, value_vectors, proj_weight, gate_scale, text_length, split_table)

    return updated
```

```python
import functools
import math

import jax
import jax.numpy as jnp
from jax import lax
from jax.experimental import pallas as pl
from jax.experimental.pallas import tpu as pltpu
from jax.sharding import PartitionSpec as P

HEAD_DIM = 128
LEAST_TEXT = 64
CHUNKS = 4
AHEAD = 2
MESH = pl.DeviceIdType.MESH


def local_kernel(
    latent, queries, key_vectors, value_vectors, proj_weight, gate_scale, text_length, split_table,
    base, arrived,
    q_buf, k_buf, v_buf, w_buf, latent_buf, gate_buf, text_buf, table_buf,
    attended, mate_send, mate_recv, kept, far_send, near_send, near_recv, own,
    q_sem, kv_sem, w_sem, small_sem, base_sem,
    mate_sems, far_sems, near_sems,
):
    seq, tp = lax.axis_index("seq"), lax.axis_index("tp")
    core = lax.rem(tp, 2)
    mate = tp + 1 - 2 * core
    far = lax.rem(tp + 2, 4)
    far_mate = lax.rem(mate + 2, 4)
    tokens, width = q_buf.shape
    block = tokens // 4
    heads = width // HEAD_DIM
    columns = w_buf.shape[2]

    barrier = pltpu.get_barrier_semaphore()
    for other in (mate, far):
        pl.semaphore_signal(barrier, inc=1, device_id=(seq, other), device_id_type=MESH)

    q_copies = []
    for place, owner in enumerate((far_mate, far, mate, tp)):
        q_copies.append(
            pltpu.make_async_copy(
                queries.at[pl.ds(pl.multiple_of(owner * block, block), block)],
                q_buf.at[pl.ds(place * block, block)],
                q_sem.at[place],
            )
        )
    k_copy = pltpu.make_async_copy(key_vectors, k_buf, kv_sem.at[0])
    v_copies = [
        pltpu.make_async_copy(
            value_vectors.at[:, pl.ds(head * HEAD_DIM, HEAD_DIM)],
            v_buf.at[:, pl.ds(2 * head * HEAD_DIM, HEAD_DIM)],
            kv_sem.at[1 + head],
        )
        for head in range(heads)
    ]
    table_copy = pltpu.make_async_copy(split_table, table_buf, small_sem.at[0])
    text_copy = pltpu.make_async_copy(text_length, text_buf, small_sem.at[1])
    gate_copy = pltpu.make_async_copy(gate_scale, gate_buf, small_sem.at[2])
    latent_copy = pltpu.make_async_copy(latent, latent_buf, small_sem.at[3])
    w_copies = [
        pltpu.make_async_copy(proj_weight.at[:, pl.ds(i * columns, columns)], w_buf.at[i], w_sem.at[i])
        for i in range(CHUNKS)
    ]
    for copy in (table_copy, *q_copies, k_copy, *v_copies, text_copy, gate_copy, *w_copies, latent_copy):
        copy.start()

    def remote(source, target, sems, i, other):
        return pltpu.make_async_remote_copy(
            src_ref=source.at[i],
            dst_ref=target,
            send_sem=sems.at[0, i],
            recv_sem=sems.at[1, i],
            device_id=(seq, other),
            device_id_type=MESH,
        )

    parts = [pl.ds(i * columns, columns) for i in range(CHUNKS)]
    to_mate = [remote(mate_send, mate_recv.at[i], mate_sems, i, mate) for i in range(CHUNKS)]
    to_far = [remote(far_send, arrived.at[:, parts[i]], far_sems, i, far) for i in range(CHUNKS)]
    to_owner = [remote(near_send, near_recv.at[i], near_sems, i, mate) for i in range(CHUNKS)]
    base_copies = [
        pltpu.make_async_copy(own.at[i], base.at[:, parts[i]], base_sem.at[i]) for i in range(CHUNKS)
    ]

    for head in range(heads):
        v_buf[:, pl.ds((2 * head + 1) * HEAD_DIM, HEAD_DIM)] = jnp.ones((tokens, HEAD_DIM), jnp.bfloat16)

    table_copy.wait()
    count = table_buf[seq]
    key_live = lax.broadcasted_iota(jnp.int32, (1, tokens), 1) < count
    score_scale = math.log2(math.e) / math.sqrt(HEAD_DIM)

    def attend(first, length):
        rows = pl.ds(first, length)
        columns_of = [pl.ds(head * HEAD_DIM, HEAD_DIM) for head in range(heads)]
        scores = [
            lax.dot_general(
                q_buf[rows, part], k_buf[:, part], (((1,), (1,)), ((), ())),
                preferred_element_type=jnp.float32,
            )
            for part in columns_of
        ]
        scores = [jnp.where(key_live, one * score_scale, -1e30) for one in scores]
        weights = [jnp.exp2(one - jnp.max(one, axis=1, keepdims=True)) for one in scores]
        summed = [
            jnp.dot(
                one.astype(jnp.bfloat16), v_buf[:, pl.ds(2 * head * HEAD_DIM, 2 * HEAD_DIM)],
                preferred_element_type=jnp.float32,
            )
            for head, one in enumerate(weights)
        ]
        for part, one in zip(columns_of, summed):
            attended[rows, part] = (one[:, :HEAD_DIM] / one[:, HEAD_DIM:]).astype(jnp.bfloat16)

    k_copy.wait()
    for copy in q_copies:
        copy.wait()
    for copy in v_copies:
        copy.wait()
    def send_to_mate(i, share):
        mate_send[i] = share.astype(jnp.bfloat16)

        @pl.when(tp != 3)
        def _():
            to_mate[i].start()

    def product(first, length, i):
        return jnp.dot(
            attended[pl.ds(first, length), :], w_buf[i], preferred_element_type=jnp.float32
        )

    attend(0, block)
    pl.semaphore_wait(barrier, 2)
    for i in range(AHEAD):
        w_copies[i].wait()
        send_to_mate(i, product(0, block, i))
    attend(block, block)

    text_copy.wait()
    gate_copy.wait()
    text = text_buf[seq]

    def image(owner):
        position = owner * block + lax.broadcasted_iota(jnp.int32, (block, 1), 0)
        return (position >= text) & (position < count)

    far_image = image(far)
    for i in range(CHUNKS):
        if i < AHEAD:
            kept[i] = product(block, block, i)

        @pl.when(tp != 2)
        def _():
            to_mate[i].wait_recv()
            summed = kept[i] + mate_recv[i].astype(jnp.float32)
            gated = gate_buf[pl.ds(seq, 1), parts[i]] * summed
            far_send[i] = jnp.where(far_image, gated, 0.0).astype(jnp.bfloat16)
            to_far[i].start()

        later = i + AHEAD
        if later < CHUNKS:
            w_copies[later].wait()
            share = product(0, 2 * block, later)
            kept[later] = share[block:]
            send_to_mate(later, share[:block])

    attend(2 * block, 2 * block)
    for i in range(CHUNKS):
        share = jnp.dot(
            attended[pl.ds(2 * block, 2 * block), :], w_buf[i], preferred_element_type=jnp.float32
        )
        near_send[i] = share[:block].astype(jnp.bfloat16)
        own[i] = share[block:]

        @pl.when(tp != 1)
        def _():
            to_owner[i].start()

    latent_copy.wait()
    near_image = image(tp)

    @pl.when(tp == 0)
    def _():
        near_recv[...] = jnp.zeros_like(near_recv)
        zero_copies = [
            pltpu.make_async_copy(near_recv.at[i], arrived.at[:, parts[i]], far_sems.at[1, i])
            for i in range(CHUNKS)
        ]
        for i in range(CHUNKS):
            zero_copies[i].start()
            own[i] = latent_buf[:, parts[i]].astype(jnp.float32)
            base_copies[i].start()
        for copy in zero_copies:
            copy.wait()

    @pl.when(tp != 0)
    def _():
        for i in range(CHUNKS):
            to_owner[i].wait_recv()
            projected = own[i] + near_recv[i].astype(jnp.float32)
            residual = latent_buf[:, parts[i]].astype(jnp.float32)
            gate = gate_buf[pl.ds(seq, 1), parts[i]]
            own[i] = jnp.where(near_image, residual + gate * projected, residual)
            base_copies[i].start()
        for i in range(CHUNKS):
            to_far[i].wait_recv()

    for copy in base_copies:
        copy.wait()
    for copies, idle in ((to_mate, 3), (to_far, 2), (to_owner, 1)):

        @pl.when(tp != idle)
        def _():
            for copy in copies:
                copy.wait_send()


def on_device_local(
    latent, queries, key_vectors, value_vectors, proj_weight, gate_scale, text_length, split_table
):
    tokens, width = queries.shape
    model = proj_weight.shape[1]
    block, columns = tokens // 4, model // CHUNKS
    in_hbm = pl.BlockSpec(memory_space=pltpu.HBM)
    blocks16 = pltpu.VMEM((CHUNKS, block, columns), jnp.bfloat16)
    blocks32 = pltpu.VMEM((CHUNKS, block, columns), jnp.float32)
    base, arrived = pl.pallas_call(
        local_kernel,
        out_shape=(
            jax.ShapeDtypeStruct(latent.shape, jnp.float32),
            jax.ShapeDtypeStruct(latent.shape, jnp.bfloat16),
        ),
        in_specs=[in_hbm] * 8,
        out_specs=(in_hbm, in_hbm),
        scratch_shapes=[
            pltpu.VMEM((tokens, width), jnp.bfloat16),
            pltpu.VMEM((tokens, width), jnp.bfloat16),
            pltpu.VMEM((tokens, 2 * width), jnp.bfloat16),
            pltpu.VMEM((CHUNKS, width, columns), jnp.bfloat16),
            pltpu.VMEM(latent.shape, jnp.bfloat16),
            pltpu.VMEM(gate_scale.shape, jnp.float32),
            pltpu.SMEM(text_length.shape, jnp.int32),
            pltpu.SMEM((split_table.size,), jnp.int32),
            pltpu.VMEM((tokens, width), jnp.bfloat16),
            blocks16, blocks16, blocks32, blocks16, blocks16, blocks16, blocks32,
            pltpu.SemaphoreType.DMA((4,)),
            pltpu.SemaphoreType.DMA((1 + width // HEAD_DIM,)),
            pltpu.SemaphoreType.DMA((CHUNKS,)),
            pltpu.SemaphoreType.DMA((4,)),
            pltpu.SemaphoreType.DMA((CHUNKS,)),
            pltpu.SemaphoreType.DMA((2, CHUNKS)),
            pltpu.SemaphoreType.DMA((2, CHUNKS)),
            pltpu.SemaphoreType.DMA((2, CHUNKS)),
        ],
        compiler_params=pltpu.CompilerParams(
            collective_id=0, has_side_effects=True, vmem_limit_bytes=64 * 2**20
        ),
        cost_estimate=pl.CostEstimate(
            flops=2 * tokens * width * (model + 2 * tokens), bytes_accessed=4 * 2**20, transcendentals=0
        ),
    )(latent, queries, key_vectors, value_vectors, proj_weight, gate_scale, text_length, split_table.reshape(-1))
    return (base + arrived.astype(jnp.float32)).astype(jnp.bfloat16)


def shortened(shard):
    return jax.tree.map(lambda a: a.astype(jnp.bfloat16) if a.dtype == jnp.float32 else a, shard)


def from_partner(block, axis, stride):
    count = lax.axis_size(axis)
    route = []
    for low in range(count):
        high = low | 1 << stride
        if high != low and high < count:
            route += [(low, high), (high, low)]
    return lax.ppermute(block, axis, route)


def hop_block(moving, bit_number):
    return jax.tree.map(
        lambda part, own: part.astype(own.dtype),
        from_partner(shortened(moving), "seq", bit_number),
        moving,
    )


def on_device(
    latent, queries, key_vectors, value_vectors, proj_weight, gate_scale, text_length, split_table
):
    group_size = split_table.shape[1]
    tokens = queries.shape[0]
    feature_width = queries.shape[1]
    head_count = feature_width // HEAD_DIM
    seq_index = lax.axis_index("seq")
    item_index = seq_index // group_size
    group_place = seq_index % group_size
    counts = lax.dynamic_index_in_dim(split_table, item_index, 0, keepdims=False)
    members = jnp.arange(group_size, dtype=jnp.int32)
    offset = jnp.sum(jnp.where(members < group_place, counts, 0))
    own_count = jnp.sum(jnp.where(members == group_place, counts, 0))
    slot_index = jnp.arange(tokens, dtype=jnp.int32)
    query_live = slot_index < own_count
    text_count = jnp.sum(
        jnp.where(jnp.arange(text_length.shape[0], dtype=jnp.int32) == item_index, text_length, 0)
    )
    image_mask = query_live & (offset + slot_index >= text_count)
    query_heads = queries.reshape(tokens, head_count, HEAD_DIM)
    score_scale = 1.0 / math.sqrt(HEAD_DIM)

    def absorb(softmax_carry, stacked, key_live):
        running_max, running_sum, running_acc = softmax_carry
        length = stacked.shape[1]
        key_heads = stacked[0].reshape(length, head_count, HEAD_DIM)
        value_heads = stacked[1].reshape(length, head_count, HEAD_DIM)
        scores = (
            jnp.einsum("qhd,khd->qhk", query_heads, key_heads, preferred_element_type=jnp.float32)
            * score_scale
        )
        scores = jnp.where(key_live[None, None, :], scores, -1e30)
        new_max = jnp.maximum(running_max, jnp.max(scores, axis=2))
        shrink = jnp.exp(running_max - new_max)
        weights = jnp.exp(scores - new_max[:, :, None]) * key_live[None, None, :].astype(
            jnp.float32
        )
        running_sum = running_sum * shrink + jnp.sum(weights, axis=2)
        running_acc = running_acc * shrink[:, :, None] + jnp.einsum(
            "qhk,khd->qhd",
            weights.astype(jnp.bfloat16),
            value_heads,
            preferred_element_type=jnp.float32,
        )
        return (new_max, running_sum, running_acc)

    stacked = jnp.stack([key_vectors, value_vectors])
    softmax_carry = (
        jnp.full((tokens, head_count), -1e30, jnp.float32),
        jnp.zeros((tokens, head_count), jnp.float32),
        jnp.zeros((tokens, head_count, HEAD_DIM), jnp.float32),
    )
    softmax_carry = absorb(softmax_carry, stacked, query_live)
    if group_size > 1:
        bit_total = group_size.bit_length() - 1

        def make_branch(bit_number):

            def branch(moving):
                return hop_block(moving, bit_number)

            return branch

        branch_list = [make_branch(bit_number) for bit_number in range(bit_total)]

        def cycle_step(step_index, loop_carry):
            inner_carry, moving = loop_carry
            trailing = jnp.int32(0)
            for bit_number in range(bit_total - 1):
                trailing = trailing + (step_index % (2 << bit_number) == 0).astype(jnp.int32)
            moving = lax.switch(trailing, branch_list, moving)
            anchor = jnp.bitwise_xor(group_place, jnp.bitwise_xor(step_index, step_index // 2))
            anchor_count = jnp.sum(jnp.where(members == anchor, counts, 0))
            return (absorb(inner_carry, moving, slot_index < anchor_count), moving)

        softmax_carry, moving = lax.fori_loop(1, group_size, cycle_step, (softmax_carry, stacked))
    running_max, running_sum, running_acc = softmax_carry
    attended = (
        (running_acc / running_sum[:, :, None]).reshape(tokens, feature_width).astype(jnp.bfloat16)
    )
    row_share = tokens // lax.axis_size("tp")
    projected = lax.psum_scatter(
        jnp.dot(attended, proj_weight, preferred_element_type=jnp.float32).astype(jnp.bfloat16),
        "tp",
        scatter_dimension=0,
        tiled=True,
    ).astype(jnp.float32)
    tp_first = lax.axis_index("tp") * row_share
    my_image = lax.dynamic_slice_in_dim(image_mask, tp_first, row_share, 0)
    gate_row = lax.dynamic_index_in_dim(gate_scale, item_index, 0, keepdims=False)
    residual_base = latent.astype(jnp.float32)
    return jnp.where(
        my_image[:, None], residual_base + gate_row[None, :] * projected, residual_base
    ).astype(jnp.bfloat16)


def solution(mesh):
    in_specs = (
        P(("seq", "tp"), None),
        P("seq", "tp"),
        P("seq", "tp"),
        P("seq", "tp"),
        P("tp", None),
        P(),
        P(),
        P(),
    )
    out_specs = P(("seq", "tp"), None)

    def updated(
        latent, queries, key_vectors, value_vectors, proj_weight, gate_scale, text_length, split_table
    ):
        tokens = queries.shape[0] // mesh.shape["seq"]
        whole_request = split_table.shape[1] == 1
        text_first = mesh.shape["tp"] == 4 and tokens // 4 <= LEAST_TEXT
        return jax.shard_map(
            on_device_local if whole_request and text_first else on_device,
            mesh=mesh, in_specs=in_specs, out_specs=out_specs, check_vma=False,
        )(latent, queries, key_vectors, value_vectors, proj_weight, gate_scale, text_length, split_table)

    return updated
```
